768 devices in a mesh: owner: 48 (over z, x), reader: 16 (over y, core).
Axes of the slice: x: 4, y: 8, z: 12, core: 2. Of those that a mesh axis runs over, the one named last changes fastest.
Arguments:
- table: float32 [49152, 128], P('owner'), may hold values from -3 to 3
- accum: float32 [49152], P('owner'), may hold values from 0.001 to 0.1
- serve: int32 [48, 16, 48, 128], P('owner', 'reader'), may hold values from 0 to 1023, as said below
- counts: int32 [48, 16, 48], P('owner', 'reader'), may hold values from 16 to 128, as said below
- slot_map: int32 [48, 16, 6144], P('owner', 'reader'), may hold values from 0 to 6143, each once within a row
- bag_rows: int32 [196608, 4, 8], P(('owner', 'reader')), may hold values from 0 to 6143
- bag_len: int32 [196608, 4], P(('owner', 'reader')), may hold values from 1 to 8
- labels: int32 [196608], P(('owner', 'reader')), may hold values 0 or 1
- w1: bfloat16 [512, 1024], replicated, may hold values from -0.25 to 0.25
- b1: float32 [1024], replicated, may hold values from -3 to 3
- w2: bfloat16 [1024], replicated, may hold values from -0.1875 to 0.1875
Outputs:
- new_table: float32 [49152, 128], P('owner')
- new_accum: float32 [49152], P('owner')
- row_grad: float32 [49152, 128], P('owner')
- w1_grad: float32 [512, 1024], replicated
- w2_grad: float32 [1024], replicated
- logits: float32 [196608], P(('owner', 'reader'))
The draws below stay inside these ranges and needn't reach their ends.
Inputs may be any that keep to these rules, and one draw needn't show every extreme that they name: serve[o, r, p, s] is a row number of owner index o, 0 to 1023, and equal for r and r + 1 with r even. counts are equal for r and r + 1 with r even; each (o, r) has some p with a full block. Each slot_map[p, r] is a permutation of 0 to 6143.
All inputs are finite; a program needn't handle non-finite values. No bound on the sum of `labels` on one device may be relied on, other than what follows from the above.
Results may differ from the reference program's by a relative error of at most 0.0043.
Values may be sent and summed in bfloat16 or wider, within the bound.
No kernel may reach another device: no remote copies, remote signals or barrier semaphores. Data moves between devices by JAX's collectives and lax.ppermute only.
A program may use at most 64 MiB of HBM per device.

```python
import math
import jax
import jax.numpy as jnp
from jax import lax

E = 128
H = 1024
NF = 4
BAG = 8
SLOTS = 128
BATCH_DEV = 256
RDEV = 1024
BATCH = 196608
ROWS = 49152
CACHE = 6144
N_OWNER = 48
N_READER = 16


def draw_serve(key, part):
    key = jax.random.fold_in(key, 11)
    halves = jax.random.randint(key, (N_OWNER, N_READER // 2, N_OWNER, SLOTS), 0, RDEV)
    halves = halves.at[:, :, 0, 0].set(RDEV - 1)
    halves = halves.at[:, :, 0, 1].set(0)
    return jnp.repeat(halves, 2, axis=1).astype(jnp.int32)


def draw_counts(key, part):
    key = jax.random.fold_in(key, 12)
    first_key, second_key = jax.random.split(key)
    filled = jax.random.randint(first_key, (N_OWNER, N_READER // 2, N_OWNER), SLOTS // 8, SLOTS + 1)
    chosen = jax.random.randint(second_key, (N_OWNER, N_READER // 2), 0, N_OWNER)
    hits = jnp.arange(N_OWNER, dtype=jnp.int32)[None, None, :] == chosen[:, :, None]
    filled = jnp.where(hits, SLOTS, filled)
    return jnp.repeat(filled, 2, axis=1).astype(jnp.int32)


def touch_ends(values, stream_key, low, high):
    place = [jax.random.randint(jax.random.fold_in(stream_key, axis), (), 0, length) for axis, length in enumerate(values.shape)]
    main_axis = values.shape.index(max(values.shape))
    neighbour = place[:main_axis] + [(place[main_axis] + 1) % values.shape[main_axis]] + place[main_axis + 1:]
    return values.at[tuple(place)].set(low).at[tuple(neighbour)].set(high)


def levels(own_key, extent, cuts, smallest, largest):
    factor_of = 1.0
    for dim, parts in cuts:
        steps = jax.random.uniform(jax.random.fold_in(jax.random.fold_in(own_key, 6), dim), (parts,), jnp.float32, smallest / len(cuts), largest / len(cuts))
        factor_of = factor_of * jnp.repeat(jnp.exp(steps), extent[dim] // parts).reshape((-1,) + (1,) * (len(extent) - 1 - dim))
    return factor_of


def noise(rng, dims, deviation, bound, shards=(), held_as=jnp.bfloat16):
    loudness = levels(rng, dims, shards, -0.22, 0.18) if shards else 1.0
    drawn = jax.random.normal(rng, dims, jnp.float32) * deviation * loudness
    return jnp.minimum(jnp.maximum(drawn, -bound), bound).astype(held_as)


def setup_inputs(seed: int = 0) -> dict:
    keys = jax.random.split(jax.random.key(seed), 12)
    return {
        "table": noise(keys[0], (ROWS, E), 0.5, 3.0, ((0, 48),), jnp.float32),
        "accum": jnp.clip(jnp.exp(math.log(0.1) - 4.6051702 * jax.random.uniform(keys[1], (ROWS,), jnp.float32) ** levels(keys[1], (ROWS,), ((0, 48),), -0.2, 0.2)), 0.001, 0.1),
        "serve": draw_serve(jax.random.fold_in(keys[11], 71), 0),
        "counts": draw_counts(jax.random.fold_in(keys[11], 71), 0),
        "slot_map": jax.vmap(lambda own: jax.random.permutation(own, CACHE))(jax.random.split(keys[4], N_OWNER * N_READER)).reshape((N_OWNER, N_READER, CACHE)).astype(jnp.int32),
        "bag_rows": touch_ends(jax.random.randint(keys[5], (BATCH, NF, BAG), 0, CACHE), jax.random.fold_in(keys[5], 1), 0, CACHE - 1).astype(jnp.int32),
        "bag_len": touch_ends(jax.random.randint(keys[6], (BATCH, NF), 1, BAG + 1), jax.random.fold_in(keys[6], 1), 1, BAG).astype(jnp.int32),
        "labels": touch_ends((jax.random.randint(keys[7], (BATCH,), 0, 2) < 1).astype(jnp.int32), jax.random.fold_in(keys[7], 1), 0, 1),
        "w1": noise(keys[8], (NF * E, H), (NF * E) ** -0.5, 0.25),
        "b1": noise(keys[9], (H,), 0.5, 3.0, (), jnp.float32),
        "w2": noise(keys[10], (H,), H ** -0.5, 0.1875),
    }


LEARN_RATE = 0.05

def reference(table, accum, serve, counts, slot_map, bag_rows, bag_len, labels, w1, b1, w2):
    devices = N_OWNER * N_READER
    cache_size = N_OWNER * SLOTS
    base = (jnp.arange(N_OWNER, dtype=jnp.int32) * jnp.int32(RDEV))[:, None]
    slot_iota = jnp.arange(SLOTS, dtype=jnp.int32)
    depth_iota = jnp.arange(BAG, dtype=jnp.int32)
    w2_wide = w2.astype(jnp.float32)
    b1_wide = b1.astype(jnp.float32)
    table_wide = table.astype(jnp.float32)

    def one_device(carry, device):
        grad_w1, grad_w2, grads = carry
        owner_p = (device // N_READER).astype(jnp.int32)
        reader_r = (device % N_READER).astype(jnp.int32)
        lists = serve[:, reader_r, owner_p, :].astype(jnp.int32)
        limits = counts[:, reader_r, owner_p].astype(jnp.int32)
        valid = (slot_iota[None, :] < limits[:, None]).reshape(-1)
        index = (base + lists).reshape(-1).astype(jnp.int32)
        fetched = jnp.where(valid[:, None], table_wide[index], jnp.zeros((), jnp.float32)).astype(jnp.bfloat16)
        places = slot_map[owner_p, reader_r].astype(jnp.int32)
        source = jnp.zeros((cache_size,), jnp.int32).at[places].set(jnp.arange(cache_size, dtype=jnp.int32))
        start = (device * jnp.int32(BATCH_DEV)).astype(jnp.int32)
        bags = lax.dynamic_slice_in_dim(bag_rows, start, BATCH_DEV, 0).astype(jnp.int32)
        lengths = lax.dynamic_slice_in_dim(bag_len, start, BATCH_DEV, 0).astype(jnp.int32)
        marks = lax.dynamic_slice_in_dim(labels, start, BATCH_DEV, 0)
        entries = source[bags].astype(jnp.int32)
        inside = depth_iota[None, None, :] < lengths[:, :, None]
        gathered = fetched[entries].astype(jnp.float32)
        pooled = lax.optimization_barrier(jnp.sum(jnp.where(inside[..., None], gathered, jnp.zeros((), jnp.float32)), axis=2))
        pooled = pooled.reshape(BATCH_DEV, NF * E).astype(jnp.bfloat16)
        pre = jnp.dot(pooled, w1, preferred_element_type=jnp.float32) + b1_wide
        sig_pre = jax.nn.sigmoid(pre)
        active = pre * sig_pre
        logits = jnp.dot(active, w2_wide, precision=lax.Precision.HIGHEST).astype(jnp.float32)
        error = (jax.nn.sigmoid(logits) - marks.astype(jnp.float32)).astype(jnp.float32)
        part_w2 = jnp.dot(error, active, precision=lax.Precision.HIGHEST)
        slope = sig_pre * (1.0 + pre * (1.0 - sig_pre))
        grad_pre = (error[:, None] * w2_wide[None, :] * slope).astype(jnp.bfloat16)
        part_w1 = jnp.dot(pooled.T, grad_pre, preferred_element_type=jnp.float32)
        grad_pooled = jnp.dot(grad_pre, w1.T, preferred_element_type=jnp.float32)
        terms = jnp.where(inside[..., None], grad_pooled.reshape(BATCH_DEV, NF, 1, E), jnp.zeros((), jnp.float32))
        slot_grad = jax.ops.segment_sum(terms.reshape(-1, E), entries.reshape(-1), num_segments=cache_size)
        added = jnp.where(valid[:, None], slot_grad, jnp.zeros((), jnp.float32)).astype(grads.dtype)
        grads = grads.at[index].add(added)
        new_w1 = grad_w1 + part_w1.astype(grad_w1.dtype)
        new_w2 = grad_w2 + part_w2.astype(grad_w2.dtype)
        return ((new_w1, new_w2, grads), logits)
    init = (jnp.zeros((NF * E, H), jnp.float32), jnp.zeros((H,), jnp.float32), jnp.zeros((N_OWNER * RDEV, E), jnp.float32))
    (w1_grad, w2_grad, row_grad), logits = lax.scan(one_device, init, jnp.arange(devices, dtype=jnp.int32))
    new_accum = accum.astype(jnp.float32) + lax.optimization_barrier(jnp.mean(row_grad * row_grad, axis=1))
    new_table = table_wide - LEARN_RATE * row_grad / jnp.sqrt(new_accum)[:, None]
    return (new_table, new_accum, row_grad, w1_grad, w2_grad, logits.reshape(-1))
```

```python
import functools

import jax
import jax.numpy as jnp
from jax import lax
from jax.experimental import pallas as pl
from jax.experimental.pallas import tpu as pltpu
from jax.sharding import PartitionSpec as P

LEARN_RATE = 0.05
LANES = 128
bf16 = jnp.bfloat16
f32 = jnp.float32
VMEM = pl.BlockSpec(memory_space=pltpu.VMEM)
PARAMS = pltpu.CompilerParams(vmem_limit_bytes=48 * 1024 * 1024)


def fetch_kernel(slot_ref, table_ref, out_ref):
    table = table_ref[...].astype(bf16)
    rows = lax.broadcasted_iota(jnp.int32, (LANES, table.shape[0]), 1)
    for k in range(slot_ref.shape[1]):
        hot = jnp.where(slot_ref[:, k : k + 1] == rows, 1.0, 0.0).astype(bf16)
        picked = jnp.dot(hot, table, preferred_element_type=f32)
        out_ref[k * LANES : (k + 1) * LANES, :] = picked.astype(bf16)


def fetch(slot_cols, table):
    slots = slot_cols.shape[1] * LANES
    return pl.pallas_call(
        fetch_kernel,
        out_shape=jax.ShapeDtypeStruct((slots, table.shape[1]), bf16),
        in_specs=[VMEM] * 2,
        out_specs=VMEM,
        compiler_params=PARAMS,
        name="fetch",
    )(slot_cols, table)


def row_sum_kernel(slot_ref, value_ref, out_ref):
    n = out_ref.shape[0]
    iota = lax.broadcasted_iota(jnp.int32, (n, LANES), 0)
    total = jnp.zeros(out_ref.shape, f32)
    for k in range(0, slot_ref.shape[0], 2):
        hot = jnp.concatenate(
            [jnp.where(slot_ref[j : j + 1, :] == iota, 1.0, 0.0).astype(bf16) for j in (k, k + 1)],
            axis=1,
        )
        values = value_ref[k * LANES : (k + 2) * LANES, :]
        total = total + jnp.dot(hot, values, preferred_element_type=f32)
    out_ref[...] = total.astype(out_ref.dtype)


def row_sum(slot_rows, values, n):
    return pl.pallas_call(
        row_sum_kernel,
        out_shape=jax.ShapeDtypeStruct((n, values.shape[1]), bf16),
        in_specs=[VMEM] * 2,
        out_specs=VMEM,
        compiler_params=PARAMS,
        name="row_sum",
    )(slot_rows, values)


def count_kernel(bag_ref, place_ref, out_ref):
    group = 16
    one, zero = jnp.ones((), bf16), jnp.zeros((), bf16)

    def step(g, carry):
        rows = pl.ds(pl.multiple_of(g * group, group), group)
        bags = bag_ref[rows, :]
        names = [
            jnp.broadcast_to(bags[:, l : l + 1], (group, LANES)).astype(jnp.int16)
            for l in range(bags.shape[1])
        ]
        for t in range(out_ref.shape[1] // LANES):
            cols = slice(t * LANES, (t + 1) * LANES)
            place = jnp.broadcast_to(place_ref[0, :, cols], (group, LANES)).astype(jnp.int16)
            total = jnp.zeros((group, LANES), bf16)
            for name in names:
                total = total + jnp.where(name == place, one, zero)
            out_ref[rows, cols] = total
        return carry

    lax.fori_loop(0, out_ref.shape[0] // group, step, 0)


def count(bags, places):
    n_bags, depth = bags.shape
    sides, _, slots = places.shape
    block = 128
    per = n_bags // sides // block
    return pl.pallas_call(
        count_kernel,
        grid=(n_bags // block,),
        out_shape=jax.ShapeDtypeStruct((n_bags, slots), bf16),
        in_specs=[
            pl.BlockSpec((block, depth), lambda i: (i, 0)),
            pl.BlockSpec((1, 1, slots), lambda i: (i // per, 0, 0)),
        ],
        out_specs=pl.BlockSpec((block, slots), lambda i: (i, 0)),
        compiler_params=PARAMS,
        cost_estimate=pl.CostEstimate(
            flops=n_bags * slots * depth * 2,
            bytes_accessed=n_bags * slots * 2,
            transcendentals=0,
        ),
        name="count",
    )(bags, places)


def top_kernel(own_ref, got_ref, w1_ref, b1_ref, w2_ref, label_ref, logit_ref, part_ref, g_ref):
    batch = label_ref.shape[0]
    feats = own_ref.shape[0] // batch
    spans = [slice(f * batch, (f + 1) * batch) for f in range(feats)]
    pooled = jnp.concatenate([(own_ref[s, :] + got_ref[s, :]).astype(bf16) for s in spans], axis=1)
    w1 = w1_ref[...]
    pre = jnp.dot(pooled, w1, preferred_element_type=f32) + b1_ref[...]
    sig_pre = jax.nn.sigmoid(pre)
    active = pre * sig_pre
    w2 = w2_ref[...].astype(f32)
    logits = jnp.sum(active * w2, axis=1, keepdims=True)
    logit_ref[...] = logits
    error = jax.nn.sigmoid(logits) - label_ref[...].astype(f32)
    part_w2 = jnp.sum(error * active, axis=0, keepdims=True)
    slope = sig_pre * (1.0 + pre * (1.0 - sig_pre))
    grad_pre = (error * w2 * slope).astype(bf16)
    grad_pooled = lax.dot_general(
        grad_pre, w1, (((1,), (1,)), ((), ())), preferred_element_type=f32
    )
    for f, s in enumerate(spans):
        g_ref[s, :] = grad_pooled[:, f * LANES : (f + 1) * LANES].astype(bf16)
    part_w1 = lax.dot_general(
        pooled, grad_pre, (((0,), (0,)), ((), ())), preferred_element_type=f32
    )
    chunks = part_ref.shape[0]
    depth, blocks = part_w1.shape[0] // chunks, part_w1.shape[1] // LANES
    for j in range(blocks):
        block = part_w1[:, j * LANES : (j + 1) * LANES].astype(bf16)
        part_ref[:, j * depth : (j + 1) * depth, :] = block.reshape(chunks, depth, LANES)
    part_ref[:, blocks * depth :, :] = jnp.zeros((chunks, 16, LANES), bf16)
    tail = [part_w2[:, j * LANES : (j + 1) * LANES] for j in range(blocks)]
    tail = jnp.concatenate(tail + [jnp.zeros((16 - blocks, LANES), f32)], axis=0)
    part_ref[0, blocks * depth :, :] = tail.astype(bf16)


def top(own, got, w1, b1, w2, labels, chunks):
    batch = labels.shape[0]
    depth = w1.size // chunks // LANES + 16
    return pl.pallas_call(
        top_kernel,
        out_shape=(
            jax.ShapeDtypeStruct((batch, 1), f32),
            jax.ShapeDtypeStruct((chunks, depth, LANES), bf16),
            jax.ShapeDtypeStruct(own.shape, bf16),
        ),
        in_specs=[VMEM] * 6,
        out_specs=(VMEM,) * 3,
        compiler_params=PARAMS,
        name="top",
    )(own, got, w1, b1, w2, labels)


def partner(shard):
    return lax.ppermute(shard, "reader", [(i, i ^ 1) for i in range(lax.axis_size("reader"))])


def exchange(blocks, axis):
    return lax.all_to_all(blocks, axis, split_axis=0, concat_axis=0, tiled=True)


def on_device(table, accum, serve, counts, slot_map, bag_rows, bag_len, labels, w1, b1, w2):
    lists = serve[0, 0]
    limits = counts[0, 0]
    n_peers, slots = lists.shape
    rows, width = table.shape
    half = slots // 2
    readers = lax.axis_size("reader")
    parity = lax.axis_index("reader") % 2
    own_lists = lax.dynamic_slice_in_dim(lists, parity * half, half, 1)
    own_slots = jnp.arange(half, dtype=jnp.int32)[None, :] + parity * half
    own_lists = jnp.where(own_slots < limits[:, None], own_lists, -1)
    slot_rows = own_lists.reshape(-1, LANES)
    picked = fetch(slot_rows.T, table)
    fetched = exchange(picked.reshape(n_peers, half, width), "owner").reshape(-1, width)

    batch, feats, depth = bag_rows.shape
    inside = jnp.arange(depth, dtype=jnp.int32)[None, None, :] < bag_len[:, :, None]
    bags = jnp.where(inside, bag_rows, -1).transpose(1, 0, 2).reshape(-1, depth)
    places = slot_map.reshape(n_peers, 2, half)
    own_places = lax.dynamic_slice_in_dim(places, parity, 1, 1).reshape(-1)
    other_places = lax.dynamic_slice_in_dim(places, 1 - parity, 1, 1).reshape(-1)
    sent = jnp.concatenate([bags.reshape(-1), other_places]).reshape(-1, LANES)
    came = partner(sent).reshape(-1)
    came_bags = came[: bags.size].reshape(bags.shape)
    came_places = came[bags.size :]
    counted = count(
        jnp.concatenate([bags, came_bags], axis=0),
        jnp.stack([own_places, came_places])[:, None, :],
    )

    pooled = jnp.dot(counted, fetched, preferred_element_type=f32)
    own_pooled, other_pooled = pooled[: batch * feats], pooled[batch * feats :]
    logits, part, grad_bags = top(
        own_pooled,
        partner(other_pooled),
        w1,
        b1[None, :],
        w2[None, :],
        labels[:, None],
        readers,
    )
    grad_both = jnp.concatenate([grad_bags, partner(grad_bags)], axis=0)
    slot_grad = lax.dot_general(
        counted, grad_both, (((0,), (0,)), ((), ())), preferred_element_type=f32
    ).astype(bf16)

    part = jnp.sum(exchange(part, "reader").astype(f32), axis=0)
    piece = 8
    chunk = jnp.zeros((n_peers * piece, LANES), f32).at[: part.shape[0]].set(part)
    chunk = jnp.sum(exchange(chunk.reshape(n_peers, piece, LANES), "owner"), axis=0)
    chunk = exchange(jnp.broadcast_to(chunk[None], (n_peers, piece, LANES)), "owner")
    chunk = chunk.reshape(-1, LANES)[: part.shape[0]].astype(bf16)

    returned = exchange(slot_grad.reshape(n_peers, half, width), "owner").reshape(-1, width)
    local_grad = row_sum(slot_rows, returned, rows)
    block = exchange(local_grad.reshape(readers, rows // readers, width), "reader")
    block = jnp.sum(block.astype(f32), axis=0)
    row_grad = lax.all_gather(block, "reader", axis=0, tiled=True)
    new_accum = accum + jnp.mean(row_grad * row_grad, axis=1)
    new_table = table - LEARN_RATE * row_grad / jnp.sqrt(new_accum)[:, None]

    every = exchange(jnp.broadcast_to(chunk[None], (readers,) + chunk.shape), "reader")
    hidden = w1.shape[1]
    blocks = hidden // LANES
    w1_grad = every[:, : -16, :].reshape(readers, blocks, -1, LANES).transpose(0, 2, 1, 3)
    w1_grad = w1_grad.reshape(w1.shape).astype(f32)
    w2_grad = every[0, -16 : blocks - 16, :].reshape(-1).astype(f32)
    return (new_table, new_accum, row_grad, w1_grad, w2_grad, logits.reshape(-1))


def solution(mesh):
    return jax.shard_map(
        on_device,
        mesh=mesh,
        in_specs=(
            P("owner", None),
            P("owner"),
            P("owner", "reader", None, None),
            P("owner", "reader", None),
            P("owner", "reader", None),
            P(("owner", "reader"), None, None),
            P(("owner", "reader"), None),
            P(("owner", "reader")),
            P(),
            P(),
            P(),
        ),
        out_specs=(
            P("owner", None),
            P("owner"),
            P("owner", None),
            P(),
            P(),
            P(("owner", "reader")),
        ),
        check_vma=False,
    )
```

```python
import functools

import jax
import jax.numpy as jnp
from jax import lax
from jax.experimental import pallas as pl
from jax.experimental.pallas import tpu as pltpu
from jax.sharding import PartitionSpec as P

LEARN_RATE = 0.05
LANES = 128
bf16 = jnp.bfloat16
f32 = jnp.float32
VMEM = pl.BlockSpec(memory_space=pltpu.VMEM)
PARAMS = pltpu.CompilerParams(vmem_limit_bytes=48 * 1024 * 1024)


def fetch_kernel(slot_ref, table_ref, out_ref):
    table = table_ref[...].astype(bf16)
    rows = lax.broadcasted_iota(jnp.int32, (LANES, table.shape[0]), 1)
    for k in range(slot_ref.shape[1]):
        hot = jnp.where(slot_ref[:, k : k + 1] == rows, 1.0, 0.0).astype(bf16)
        picked = jnp.dot(hot, table, preferred_element_type=f32)
        out_ref[k * LANES : (k + 1) * LANES, :] = picked.astype(bf16)


def fetch(slot_cols, table):
    slots = slot_cols.shape[1] * LANES
    return pl.pallas_call(
        fetch_kernel,
        out_shape=jax.ShapeDtypeStruct((slots, table.shape[1]), bf16),
        in_specs=[VMEM] * 2,
        out_specs=VMEM,
        compiler_params=PARAMS,
        name="fetch",
    )(slot_cols, table)


def row_sum_kernel(order, slot_ref, value_ref, out_ref):
    n = out_ref.shape[0]
    iota = lax.broadcasted_iota(jnp.int32, (n, LANES), 0)
    total = jnp.zeros(out_ref.shape, f32)
    for k in range(0, slot_ref.shape[0], 2):
        hot = jnp.concatenate(
            [jnp.where(slot_ref[j : j + 1, :] == iota, 1.0, 0.0).astype(bf16) for j in (k, k + 1)],
            axis=1,
        )
        values = value_ref[k * LANES : (k + 2) * LANES, :]
        total = total + jnp.dot(hot, values, preferred_element_type=f32)
    blocks = len(order)
    size = n // blocks
    for b, place in enumerate(order):
        out_ref[place * size : (place + 1) * size, :] = total[b * size : (b + 1) * size, :]


def row_sum(slot_rows, values, n, order):
    return pl.pallas_call(
        functools.partial(row_sum_kernel, order),
        out_shape=jax.ShapeDtypeStruct((n, values.shape[1]), f32),
        in_specs=[VMEM] * 2,
        out_specs=VMEM,
        compiler_params=PARAMS,
        name="row_sum",
    )(slot_rows, values)


def count_kernel(bag_ref, place_ref, out_ref):
    group, part = 32, 16
    one, zero = jnp.ones((), bf16), jnp.zeros((), bf16)

    def step(g, carry):
        rows = pl.ds(pl.multiple_of(g * group, group), group)
        bags = bag_ref[rows, :]
        names = [
            [
                jnp.broadcast_to(bags[p : p + part, l : l + 1], (part, LANES)).astype(jnp.int16)
                for l in range(bags.shape[1])
            ]
            for p in range(0, group, part)
        ]
        for t in range(out_ref.shape[1] // LANES):
            cols = slice(t * LANES, (t + 1) * LANES)
            place = jnp.broadcast_to(place_ref[0, :, cols], (part, LANES)).astype(jnp.int16)
            totals = []
            for part_names in names:
                total = jnp.zeros((part, LANES), bf16)
                for name in part_names:
                    total = total + jnp.where(name == place, one, zero)
                totals.append(total)
            out_ref[rows, cols] = jnp.concatenate(totals, axis=0).astype(out_ref.dtype)
        return carry

    lax.fori_loop(0, out_ref.shape[0] // group, step, 0)


def count(bags, places):
    n_bags, depth = bags.shape
    sides, _, slots = places.shape
    block = 128
    per = n_bags // sides // block
    return pl.pallas_call(
        count_kernel,
        grid=(n_bags // block,),
        out_shape=jax.ShapeDtypeStruct((n_bags, slots), jnp.float8_e4m3fn),
        in_specs=[
            pl.BlockSpec((block, depth), lambda i: (i, 0)),
            pl.BlockSpec((1, 1, slots), lambda i: (i // per, 0, 0)),
        ],
        out_specs=pl.BlockSpec((block, slots), lambda i: (i, 0)),
        compiler_params=PARAMS,
        cost_estimate=pl.CostEstimate(
            flops=n_bags * slots * depth * 2,
            bytes_accessed=n_bags * slots,
            transcendentals=0,
        ),
        name="count",
    )(bags, places)


def top_kernel(order, own_ref, got_ref, w1_ref, b1_ref, w2_ref, label_ref, logit_ref, part_ref, g_ref):
    batch = label_ref.shape[0]
    feats = own_ref.shape[0] // batch
    spans = [slice(f * batch, (f + 1) * batch) for f in range(feats)]
    pooled = jnp.concatenate([(own_ref[s, :] + got_ref[s, :]).astype(bf16) for s in spans], axis=1)
    w1 = w1_ref[...]
    pre = jnp.dot(pooled, w1, preferred_element_type=f32) + b1_ref[...]
    sig_pre = jax.nn.sigmoid(pre)
    active = pre * sig_pre
    w2 = w2_ref[...].astype(f32)
    logits = jnp.sum(active * w2, axis=1, keepdims=True)
    logit_ref[...] = logits
    error = jax.nn.sigmoid(logits) - label_ref[...].astype(f32)
    part_w2 = jnp.sum(error * active, axis=0, keepdims=True)
    slope = sig_pre * (1.0 + pre * (1.0 - sig_pre))
    grad_pre = (error * w2 * slope).astype(bf16)
    grad_pooled = lax.dot_general(
        grad_pre, w1, (((1,), (1,)), ((), ())), preferred_element_type=f32
    )
    for f, s in enumerate(spans):
        g_ref[s, :] = grad_pooled[:, f * LANES : (f + 1) * LANES].astype(bf16)
    part_w1 = lax.dot_general(
        pooled, grad_pre, (((0,), (0,)), ((), ())), preferred_element_type=f32
    )
    depth, blocks = part_w1.shape[0] // len(order), part_w1.shape[1] // LANES
    tail = [part_w2[:, j * LANES : (j + 1) * LANES] for j in range(blocks)]
    tail = jnp.concatenate(tail + [jnp.zeros((16 - blocks, LANES), f32)], axis=0)
    for c, place in enumerate(order):
        rows = part_w1[c * depth : (c + 1) * depth, :]
        for j in range(blocks):
            part_ref[place, j * depth : (j + 1) * depth, :] = rows[:, j * LANES : (j + 1) * LANES]
        part_ref[place, blocks * depth :, :] = tail if c == 0 else jnp.zeros_like(tail)


def top(own, got, w1, b1, w2, labels, order):
    batch = labels.shape[0]
    chunks = len(order)
    depth = w1.size // chunks // LANES + 16
    return pl.pallas_call(
        functools.partial(top_kernel, order),
        out_shape=(
            jax.ShapeDtypeStruct((batch, 1), f32),
            jax.ShapeDtypeStruct((chunks, depth, LANES), f32),
            jax.ShapeDtypeStruct(own.shape, bf16),
        ),
        in_specs=[VMEM] * 6,
        out_specs=(VMEM,) * 3,
        compiler_params=PARAMS,
        name="top",
    )(own, got, w1, b1, w2, labels)


def update_kernel(
    parity_ref,
    mine_ref,
    other_ref,
    table_ref,
    accum_ref,
    accum_col_ref,
    new_table_ref,
    new_accum_ref,
    row_grad_ref,
    w1_grad_ref,
    w2_grad_ref,
):
    chips, depth, _ = mine_ref.shape
    rows, hidden = table_ref.shape[0], w1_grad_ref.shape[1]
    size, blocks = rows // (2 * chips), hidden // LANES
    chunk = w1_grad_ref.shape[0] // (2 * chips)
    first = parity_ref[0] == 0
    for y in range(chips):
        mine, other = mine_ref[y].astype(f32), other_ref[y].astype(f32)
        for c in range(2):
            got = jnp.where(first, mine, other) if c == 0 else jnp.where(first, other, mine)
            base = (chips * c + y) * chunk
            for j in range(blocks):
                w1_grad_ref[base : base + chunk, j * LANES : (j + 1) * LANES] = got[
                    j * chunk : (j + 1) * chunk, :
                ]
            if y == 0 and c == 0:
                w2_grad_ref[...] = got[blocks * chunk : blocks * chunk + blocks, :]
            base = (2 * y + c) * size
            row_grad_ref[base : base + size, :] = got[depth - size :, :]
    grad = row_grad_ref[...]
    square = grad * grad
    means = []
    for i in range(rows // LANES):
        spread = lax.dot_general(
            jnp.full((8, LANES), 1.0 / LANES, f32),
            square[i * LANES : (i + 1) * LANES, :],
            (((1,), (1,)), ((), ())),
            precision=lax.Precision.HIGHEST,
            preferred_element_type=f32,
        )
        means.append(spread[:1, :])
    new_accum_ref[...] = accum_ref[...] + jnp.concatenate(means, axis=0)
    scale = accum_col_ref[...] + jnp.mean(square, axis=1, keepdims=True)
    new_table_ref[...] = table_ref[...] - LEARN_RATE * grad / jnp.sqrt(scale)


def update(mine, other, parity, table, accum, w1_shape):
    rows, width = table.shape
    blocks = w1_shape[1] // LANES
    smem = pl.BlockSpec(memory_space=pltpu.SMEM)
    new_table, new_accum, row_grad, w1_grad, w2_grad = pl.pallas_call(
        update_kernel,
        out_shape=(
            jax.ShapeDtypeStruct(table.shape, f32),
            jax.ShapeDtypeStruct((rows // LANES, LANES), f32),
            jax.ShapeDtypeStruct(table.shape, f32),
            jax.ShapeDtypeStruct(w1_shape, f32),
            jax.ShapeDtypeStruct((blocks, LANES), f32),
        ),
        in_specs=[smem] + [VMEM] * 5,
        out_specs=(VMEM,) * 5,
        compiler_params=PARAMS,
        name="update",
    )(parity.reshape(1), mine, other, table, accum.reshape(-1, LANES), accum[:, None])
    return new_table, new_accum.reshape(-1), row_grad, w1_grad, w2_grad.reshape(-1)


def bit_reversed(i, bits):
    return sum((i >> b & 1) << (bits - 1 - b) for b in range(bits))


def swap(shard, stride):
    pairs = [(i, i ^ stride) for i in range(lax.axis_size("reader"))]
    return lax.ppermute(shard, "reader", pairs)


def halve(blocks, sent_type, strides):
    me = lax.axis_index("reader")
    for stride in strides:
        half = blocks.shape[0] // 2
        side = me // stride % 2
        kept = lax.dynamic_slice_in_dim(blocks, side * half, half, 0)
        sent = lax.dynamic_slice_in_dim(blocks, (1 - side) * half, half, 0)
        blocks = kept + swap(sent.astype(sent_type), stride).astype(f32)
    return blocks


def partner(shard):
    return swap(shard, 1)


def exchange(blocks, axis, groups=None):
    return lax.all_to_all(
        blocks, axis, split_axis=0, concat_axis=0, tiled=True, axis_index_groups=groups
    )


def on_device(table, accum, serve, counts, slot_map, bag_rows, bag_len, labels, w1, b1, w2):
    lists = serve[0, 0]
    limits = counts[0, 0]
    n_peers, slots = lists.shape
    rows, width = table.shape
    half = slots // 2
    readers = lax.axis_size("reader")
    chips, bits = readers // 2, readers.bit_length() - 1
    strides = [1 << b for b in range(bits)]
    parity = lax.axis_index("reader") % 2
    own_lists = lax.dynamic_slice_in_dim(lists, parity * half, half, 1)
    own_slots = jnp.arange(half, dtype=jnp.int32)[None, :] + parity * half
    own_lists = jnp.where(own_slots < limits[:, None], own_lists, -1)
    slot_rows = own_lists.reshape(-1, LANES)
    picked = fetch(slot_rows.T, table)
    fetched = exchange(picked.reshape(n_peers, half, width), "owner").reshape(-1, width)

    batch, feats, depth = bag_rows.shape
    inside = jnp.arange(depth, dtype=jnp.int32)[None, None, :] < bag_len[:, :, None]
    bags = jnp.where(inside, bag_rows, -1).transpose(1, 0, 2).reshape(-1, depth)
    places = slot_map.reshape(n_peers, 2, half)
    own_places = lax.dynamic_slice_in_dim(places, parity, 1, 1).reshape(-1)
    other_places = lax.dynamic_slice_in_dim(places, 1 - parity, 1, 1).reshape(-1)
    sent = jnp.concatenate([bags.reshape(-1), other_places]).reshape(-1, LANES)
    came = partner(sent).reshape(-1)
    came_bags = came[: bags.size].reshape(bags.shape)
    came_places = came[bags.size :]
    counted = count(
        jnp.concatenate([bags, came_bags], axis=0),
        jnp.stack([own_places, came_places])[:, None, :],
    )

    pooled = jnp.dot(counted.astype(bf16), fetched, preferred_element_type=f32)
    own_pooled, other_pooled = pooled[: batch * feats], pooled[batch * feats :]
    logits, part, grad_bags = top(
        own_pooled,
        partner(other_pooled),
        w1,
        b1[None, :],
        w2[None, :],
        labels[:, None],
        [c // chips * chips + bit_reversed(c % chips, bits - 1) for c in range(readers)],
    )
    grad_both = jnp.concatenate([grad_bags, partner(grad_bags)], axis=0)
    slot_grad = lax.dot_general(
        counted.astype(bf16), grad_both, (((0,), (0,)), ((), ())), preferred_element_type=f32
    ).astype(bf16)

    part = halve(part, bf16, strides[:1])
    part, slot_grad = lax.optimization_barrier((part, slot_grad))
    returned = exchange(slot_grad.reshape(n_peers, half, width), "owner").reshape(-1, width)
    part = halve(part, bf16, strides[1:])[0]
    part, returned = lax.optimization_barrier((part, returned))
    order = [bit_reversed(b, bits) for b in range(readers)]
    local_grad = row_sum(slot_rows, returned, rows, order)
    block = local_grad.reshape(readers, rows // readers, width)

    piece = 8
    depth_w = part.shape[0]
    chunk = jnp.zeros((n_peers * piece, LANES), bf16).at[:depth_w].set(part.astype(bf16))
    chunk = exchange(chunk.reshape(n_peers, piece, LANES), "owner")
    chunk = jnp.sum(chunk.astype(f32), axis=0).astype(bf16)
    block = halve(block, f32, strides[:2])
    chunk, block = lax.optimization_barrier((chunk, block))
    chunk = exchange(jnp.broadcast_to(chunk[None], (n_peers, piece, LANES)), "owner")
    chunk = chunk.reshape(-1, LANES)[:depth_w]
    block = halve(block, f32, strides[2:])
    same_core = [list(range(c, readers, 2)) for c in range(2)]
    mine = jnp.concatenate([chunk, block[0].astype(bf16)], axis=0)
    mine = jnp.broadcast_to(mine[None], (chips,) + mine.shape)
    mine = exchange(mine, "reader", same_core)
    new_table, new_accum, row_grad, w1_grad, w2_grad = update(
        mine, partner(mine), parity, table, accum, w1.shape
    )
    return (new_table, new_accum, row_grad, w1_grad, w2_grad, logits.reshape(-1))


def solution(mesh):
    return jax.shard_map(
        on_device,
        mesh=mesh,
        in_specs=(
            P("owner", None),
            P("owner"),
            P("owner", "reader", None, None),
            P("owner", "reader", None),
            P("owner", "reader", None),
            P(("owner", "reader"), None, None),
            P(("owner", "reader"), None),
            P(("owner", "reader")),
            P(),
            P(),
            P(),
        ),
        out_specs=(
            P("owner", None),
            P("owner"),
            P("owner", None),
            P(),
            P(),
            P(("owner", "reader")),
        ),
        check_vma=False,
    )
```

```python
import functools

import jax
import jax.numpy as jnp
from jax import lax
from jax.experimental import pallas as pl
from jax.experimental.pallas import tpu as pltpu
from jax.sharding import PartitionSpec as P

LEARN_RATE = 0.05
LANES = 128
NEAR = 4
bf16 = jnp.bfloat16
f32 = jnp.float32
VMEM = pl.BlockSpec(memory_space=pltpu.VMEM)
PARAMS = pltpu.CompilerParams(vmem_limit_bytes=48 * 1024 * 1024)


def fetch_kernel(side_ref, list_ref, limit_ref, table_ref, out_ref):
    table = table_ref[...].astype(bf16)
    peers = list_ref.shape[0]
    half = list_ref.shape[1] // 2
    lists = list_ref[...].T
    side = side_ref[0]
    lists = jnp.where(side == 0, lists[:half], lists[half:])
    slots = lax.broadcasted_iota(jnp.int32, (half, peers), 0) + side * half
    lists = jnp.where(slots < limit_ref[...], lists, -1)
    rows = lax.broadcasted_iota(jnp.int32, (half, table.shape[0]), 1)
    for p in range(0, peers, 2):
        hot = jnp.concatenate(
            [jnp.where(lists[:, q : q + 1] == rows, 1.0, 0.0).astype(bf16) for q in (p, p + 1)],
            axis=0,
        )
        picked = jnp.dot(hot, table, preferred_element_type=f32)
        out_ref[p * half : (p + 2) * half, :] = picked.astype(bf16)


def fetch(side, lists, limits, table):
    slots = lists.size // 2
    smem = pl.BlockSpec(memory_space=pltpu.SMEM)
    return pl.pallas_call(
        fetch_kernel,
        out_shape=jax.ShapeDtypeStruct((slots, table.shape[1]), bf16),
        in_specs=[smem] + [VMEM] * 3,
        out_specs=VMEM,
        compiler_params=PARAMS,
        name="fetch",
    )(side.reshape(1), lists, limits[None, :], table)


def row_sum_kernel(order, slot_ref, value_ref, out_ref):
    n = out_ref.shape[0]
    iota = lax.broadcasted_iota(jnp.int32, (n, LANES), 0)
    total = jnp.zeros(out_ref.shape, f32)
    for k in range(0, slot_ref.shape[0], 2):
        hot = jnp.concatenate(
            [jnp.where(slot_ref[j : j + 1, :] == iota, 1.0, 0.0).astype(bf16) for j in (k, k + 1)],
            axis=1,
        )
        values = value_ref[k * LANES : (k + 2) * LANES, :]
        total = total + jnp.dot(hot, values, preferred_element_type=f32)
    blocks = len(order)
    size = n // blocks
    for b, place in enumerate(order):
        out_ref[place * size : (place + 1) * size, :] = total[b * size : (b + 1) * size, :]


def row_sum(slot_rows, values, n, order):
    return pl.pallas_call(
        functools.partial(row_sum_kernel, order),
        out_shape=jax.ShapeDtypeStruct((n, values.shape[1]), f32),
        in_specs=[VMEM] * 2,
        out_specs=VMEM,
        compiler_params=PARAMS,
        name="row_sum",
    )(slot_rows, values)


def count_kernel(bag_ref, place_ref, out_ref):
    group, part = 32, 16
    one, zero = jnp.ones((), bf16), jnp.zeros((), bf16)

    def step(g, carry):
        rows = pl.ds(pl.multiple_of(g * group, group), group)
        bags = bag_ref[rows, :]
        names = [
            [
                jnp.broadcast_to(bags[p : p + part, l : l + 1], (part, LANES)).astype(jnp.int16)
                for l in range(bags.shape[1])
            ]
            for p in range(0, group, part)
        ]
        for t in range(out_ref.shape[1] // LANES):
            cols = slice(t * LANES, (t + 1) * LANES)
            place = jnp.broadcast_to(place_ref[0, :, cols], (part, LANES)).astype(jnp.int16)
            totals = []
            for part_names in names:
                total = jnp.zeros((part, LANES), bf16)
                for name in part_names:
                    total = total + jnp.where(name == place, one, zero)
                totals.append(total)
            out_ref[rows, cols] = jnp.concatenate(totals, axis=0).astype(out_ref.dtype)
        return carry

    lax.fori_loop(0, out_ref.shape[0] // group, step, 0)


def count(bags, places):
    n_bags, depth = bags.shape
    sides, _, slots = places.shape
    block = 128
    per = n_bags // sides // block
    return pl.pallas_call(
        count_kernel,
        grid=(n_bags // block,),
        out_shape=jax.ShapeDtypeStruct((n_bags, slots), jnp.float8_e4m3fn),
        in_specs=[
            pl.BlockSpec((block, depth), lambda i: (i, 0)),
            pl.BlockSpec((1, 1, slots), lambda i: (i // per, 0, 0)),
        ],
        out_specs=pl.BlockSpec((block, slots), lambda i: (i, 0)),
        compiler_params=PARAMS,
        cost_estimate=pl.CostEstimate(
            flops=n_bags * slots * depth * 2,
            bytes_accessed=n_bags * slots,
            transcendentals=0,
        ),
        name="count",
    )(bags, places)


def top_kernel(
    order,
    side_ref,
    here_ref,
    came_ref,
    w1_ref,
    b1_ref,
    w2_ref,
    label_ref,
    logit_ref,
    part_ref,
    g_ref,
):
    batch = logit_ref.shape[0]
    bags = here_ref.shape[0] // 2
    spans = [slice(f * batch, (f + 1) * batch) for f in range(bags // batch)]
    pooled = []
    for s in range(2):
        total = here_ref[s * bags : (s + 1) * bags, :] + came_ref[(1 - s) * bags : (2 - s) * bags, :]
        pooled.append(jnp.concatenate([total[span].astype(bf16) for span in spans], axis=1))
    pooled = jnp.concatenate(pooled, axis=0)
    w1 = w1_ref[...]
    pre = jnp.dot(pooled, w1, preferred_element_type=f32) + b1_ref[...]
    sig_pre = jax.nn.sigmoid(pre)
    active = pre * sig_pre
    w2 = w2_ref[...].astype(f32)
    logits = jnp.sum(active * w2, axis=1, keepdims=True)
    logit_ref[...] = logits[:batch]
    error = jax.nn.sigmoid(logits) - label_ref[...].astype(f32)
    part_w2 = jnp.sum(error * active, axis=0, keepdims=True)
    slope = sig_pre * (1.0 + pre * (1.0 - sig_pre))
    grad_pre = (error * w2 * slope).astype(bf16)
    grad_pooled = lax.dot_general(
        grad_pre, w1, (((1,), (1,)), ((), ())), preferred_element_type=f32
    )
    for s in range(2):
        for f, span in enumerate(spans):
            block = grad_pooled[s * batch : (s + 1) * batch, f * LANES : (f + 1) * LANES]
            g_ref[s * bags + span.start : s * bags + span.stop, :] = block.astype(bf16)
    half = pooled.shape[1] // 2
    chosen = jnp.where(side_ref[0] == 0, pooled[:, :half], pooled[:, half:])
    part_w1 = lax.dot_general(
        chosen, grad_pre, (((0,), (0,)), ((), ())), preferred_element_type=f32
    )
    depth, blocks = part_w1.shape[0] // len(order), part_w1.shape[1] // LANES
    pieces = part_ref.shape[1]
    each = blocks // pieces
    for c, place in enumerate(order):
        rows = part_w1[c * depth : (c + 1) * depth, :]
        for j in range(blocks):
            base = j % each * depth
            block = rows[:, j * LANES : (j + 1) * LANES]
            part_ref[place, j // each, base : base + depth, :] = block
        for p in range(pieces):
            part_ref[place, p, each * depth :, :] = jnp.zeros((blocks, LANES), f32)
    for j in range(blocks):
        row = each * depth + j
        part_ref[order[0], 0, row : row + 1, :] = part_w2[:, j * LANES : (j + 1) * LANES]


def top(side, here, came, w1, b1, w2, labels, order, pieces):
    batch = labels.shape[0] // 2
    chunks = len(order)
    blocks = w1.shape[1] // LANES
    depth = w1.size // 2 // chunks // pieces // LANES + blocks
    smem = pl.BlockSpec(memory_space=pltpu.SMEM)
    return pl.pallas_call(
        functools.partial(top_kernel, order),
        out_shape=(
            jax.ShapeDtypeStruct((batch, 1), f32),
            jax.ShapeDtypeStruct((chunks, pieces, depth, LANES), f32),
            jax.ShapeDtypeStruct(here.shape, bf16),
        ),
        in_specs=[smem] + [VMEM] * 6,
        out_specs=(VMEM,) * 3,
        compiler_params=PARAMS,
        name="top",
    )(side.reshape(1), here, came, w1, b1, w2, labels)


def update_kernel(
    parity_ref,
    mine_ref,
    other_ref,
    table_ref,
    accum_ref,
    accum_col_ref,
    new_table_ref,
    new_accum_ref,
    row_grad_ref,
    w1_grad_ref,
    w2_grad_ref,
):
    chips, depth, _ = mine_ref.shape
    rows, hidden = table_ref.shape[0], w1_grad_ref.shape[1]
    size, blocks = rows // (2 * chips), hidden // LANES
    each = blocks // NEAR
    chunk = w1_grad_ref.shape[0] // (2 * chips)
    first = parity_ref[0] == 0
    for y in range(chips):
        mine, other = mine_ref[y].astype(f32), other_ref[y].astype(f32)
        for c in range(2):
            got = jnp.where(first, mine, other) if c == 0 else jnp.where(first, other, mine)
            base = (chips * c + y) * chunk
            for j in range(blocks):
                at = j // each * (each * chunk + blocks) + j % each * chunk
                cols = slice(j * LANES, (j + 1) * LANES)
                w1_grad_ref[base : base + chunk, cols] = got[at : at + chunk, :]
            if y == 0 and c == 0:
                w2_grad_ref[...] = got[each * chunk : each * chunk + blocks, :]
            base = (2 * y + c) * size
            row_grad_ref[base : base + size, :] = got[depth - size :, :]
    grad = row_grad_ref[...]
    square = grad * grad
    means = []
    for i in range(rows // LANES):
        spread = lax.dot_general(
            jnp.full((8, LANES), 1.0 / LANES, f32),
            square[i * LANES : (i + 1) * LANES, :],
            (((1,), (1,)), ((), ())),
            precision=lax.Precision.HIGHEST,
            preferred_element_type=f32,
        )
        means.append(spread[:1, :])
    new_accum_ref[...] = accum_ref[...] + jnp.concatenate(means, axis=0)
    scale = accum_col_ref[...] + jnp.mean(square, axis=1, keepdims=True)
    new_table_ref[...] = table_ref[...] - LEARN_RATE * grad / jnp.sqrt(scale)


def update(mine, other, parity, table, accum, w1_shape):
    rows, width = table.shape
    blocks = w1_shape[1] // LANES
    smem = pl.BlockSpec(memory_space=pltpu.SMEM)
    new_table, new_accum, row_grad, w1_grad, w2_grad = pl.pallas_call(
        update_kernel,
        out_shape=(
            jax.ShapeDtypeStruct(table.shape, f32),
            jax.ShapeDtypeStruct((rows // LANES, LANES), f32),
            jax.ShapeDtypeStruct(table.shape, f32),
            jax.ShapeDtypeStruct(w1_shape, f32),
            jax.ShapeDtypeStruct((blocks, LANES), f32),
        ),
        in_specs=[smem] + [VMEM] * 5,
        out_specs=(VMEM,) * 5,
        compiler_params=PARAMS,
        name="update",
    )(parity.reshape(1), mine, other, table, accum.reshape(-1, LANES), accum[:, None])
    return new_table, new_accum.reshape(-1), row_grad, w1_grad, w2_grad.reshape(-1)


def bit_reversed(i, bits):
    return sum((i >> b & 1) << (bits - 1 - b) for b in range(bits))


def swap(shard, stride, axis="reader"):
    pairs = [(i, i ^ stride) for i in range(lax.axis_size(axis))]
    return lax.ppermute(shard, axis, pairs)


def halve(blocks, sent_type, strides, axis="reader"):
    me = lax.axis_index(axis)
    for stride in strides:
        half = blocks.shape[0] // 2
        side = me // stride % 2
        kept = lax.dynamic_slice_in_dim(blocks, side * half, half, 0)
        sent = lax.dynamic_slice_in_dim(blocks, (1 - side) * half, half, 0)
        blocks = kept + swap(sent.astype(sent_type), stride, axis).astype(f32)
    return blocks


def double(blocks, strides, axis):
    me = lax.axis_index(axis)
    for stride in strides:
        came = swap(blocks, stride, axis)
        low = me // stride % 2 == 0
        first, second = jnp.where(low, blocks, came), jnp.where(low, came, blocks)
        blocks = jnp.concatenate([first, second], axis=0)
    return blocks


def partner(shard):
    return swap(shard, 1)


def exchange(blocks, axis, groups=None):
    return lax.all_to_all(
        blocks, axis, split_axis=0, concat_axis=0, tiled=True, axis_index_groups=groups
    )


def on_device(table, accum, serve, counts, slot_map, bag_rows, bag_len, labels, w1, b1, w2):
    lists = serve[0, 0]
    limits = counts[0, 0]
    n_peers, slots = lists.shape
    rows, width = table.shape
    half = slots // 2
    readers = lax.axis_size("reader")
    chips, bits = readers // 2, readers.bit_length() - 1
    strides = [1 << b for b in range(bits)]
    parity = lax.axis_index("reader") % 2
    own_lists = lax.dynamic_slice_in_dim(lists, parity * half, half, 1)
    own_slots = jnp.arange(half, dtype=jnp.int32)[None, :] + parity * half
    own_lists = jnp.where(own_slots < limits[:, None], own_lists, -1)
    slot_rows = own_lists.reshape(-1, LANES)
    picked = fetch(parity, lists, limits, table)
    fetched = exchange(picked.reshape(n_peers, half, width), "owner").reshape(-1, width)

    batch, feats, depth = bag_rows.shape
    inside = jnp.arange(depth, dtype=jnp.int32)[None, None, :] < bag_len[:, :, None]
    bags = jnp.where(inside, bag_rows, -1).transpose(1, 0, 2).reshape(-1, depth)
    places = slot_map.reshape(n_peers, 2, half)
    own_places = lax.dynamic_slice_in_dim(places, parity, 1, 1).reshape(-1)
    other_places = lax.dynamic_slice_in_dim(places, 1 - parity, 1, 1).reshape(-1)
    sent = jnp.concatenate([bags.reshape(-1), other_places, labels]).reshape(-1, LANES)
    came = partner(sent).reshape(-1)
    came_bags = came[: bags.size].reshape(bags.shape)
    came_places = came[bags.size : -batch]
    both_labels = jnp.concatenate([labels, came[-batch:]])
    counted = count(
        jnp.concatenate([bags, came_bags], axis=0),
        jnp.stack([own_places, came_places])[:, None, :],
    )

    pooled = jnp.dot(counted.astype(bf16), fetched, preferred_element_type=f32)
    logits, part, grad_both = top(
        parity,
        pooled,
        partner(pooled),
        w1,
        b1[None, :],
        w2[None, :],
        both_labels[:, None],
        [bit_reversed(c, bits - 1) for c in range(chips)],
        NEAR,
    )
    slot_grad = lax.dot_general(
        counted.astype(bf16), grad_both, (((0,), (0,)), ((), ())), preferred_element_type=f32
    ).astype(bf16)

    part = halve(part, bf16, strides[1:2])
    part, slot_grad = lax.optimization_barrier((part, slot_grad))
    returned = exchange(slot_grad.reshape(n_peers, half, width), "owner").reshape(-1, width)
    part = halve(part, bf16, strides[2:])[0]
    part = halve(part, f32, [1, 2], "owner")[0].astype(bf16)
    part, returned = lax.optimization_barrier((part, returned))
    order = [b % 2 * chips + b // 2 for b in range(readers)]
    local_grad = row_sum(slot_rows, returned, rows, order)
    block = local_grad.reshape(readers, rows // readers, width)

    far = n_peers // NEAR
    part = jnp.broadcast_to(part[None], (far,) + part.shape)
    part = exchange(part, "owner", [list(range(x, n_peers, NEAR)) for x in range(NEAR)])
    chunk = jnp.sum(part.astype(f32), axis=0, keepdims=True).astype(bf16)
    block = halve(block, f32, strides[:1])
    chunk, block = lax.optimization_barrier((chunk, block))
    same_core = [list(range(c, readers, 2)) for c in range(2)]
    block = jnp.sum(exchange(block, "reader", same_core), axis=0)
    chunk = double(chunk, [2, 1], "owner").reshape(-1, LANES)
    mine = jnp.concatenate([chunk, block.astype(bf16)], axis=0)
    mine = jnp.broadcast_to(mine[None], (chips,) + mine.shape)
    mine = exchange(mine, "reader", same_core)
    new_table, new_accum, row_grad, w1_grad, w2_grad = update(
        mine, partner(mine), parity, table, accum, w1.shape
    )
    return (new_table, new_accum, row_grad, w1_grad, w2_grad, logits.reshape(-1))


def solution(mesh):
    return jax.shard_map(
        on_device,
        mesh=mesh,
        in_specs=(
            P("owner", None),
            P("owner"),
            P("owner", "reader", None, None),
            P("owner", "reader", None),
            P("owner", "reader", None),
            P(("owner", "reader"), None, None),
            P(("owner", "reader"), None),
            P(("owner", "reader")),
            P(),
            P(),
            P(),
        ),
        out_specs=(
            P("owner", None),
            P("owner"),
            P("owner", None),
            P(),
            P(),
            P(("owner", "reader")),
        ),
        check_vma=False,
    )
```

```python
import functools

import jax
import jax.numpy as jnp
from jax import lax
from jax.experimental import pallas as pl
from jax.experimental.pallas import tpu as pltpu
from jax.sharding import PartitionSpec as P

LEARN_RATE = 0.05
LANES = 128
NEAR = 4
bf16 = jnp.bfloat16
f32 = jnp.float32
VMEM = pl.BlockSpec(memory_space=pltpu.VMEM)
PARAMS = pltpu.CompilerParams(vmem_limit_bytes=48 * 1024 * 1024)


def fetch_kernel(side_ref, list_ref, limit_ref, table_ref, out_ref):
    table = table_ref[...].astype(bf16)
    peers = list_ref.shape[0]
    half = list_ref.shape[1] // 2
    lists = list_ref[...].T
    side = side_ref[0]
    lists = jnp.where(side == 0, lists[:half], lists[half:])
    slots = lax.broadcasted_iota(jnp.int32, (half, peers), 0) + side * half
    lists = jnp.where(slots < limit_ref[...], lists, -1)
    rows = lax.broadcasted_iota(jnp.int32, (half, table.shape[0]), 1)
    for p in range(0, peers, 2):
        hot = jnp.concatenate(
            [jnp.where(lists[:, q : q + 1] == rows, 1.0, 0.0).astype(bf16) for q in (p, p + 1)],
            axis=0,
        )
        picked = jnp.dot(hot, table, preferred_element_type=f32)
        out_ref[p * half : (p + 2) * half, :] = picked.astype(bf16)


def fetch(side, lists, limits, table):
    slots = lists.size // 2
    smem = pl.BlockSpec(memory_space=pltpu.SMEM)
    return pl.pallas_call(
        fetch_kernel,
        out_shape=jax.ShapeDtypeStruct((slots, table.shape[1]), bf16),
        in_specs=[smem] + [VMEM] * 3,
        out_specs=VMEM,
        compiler_params=PARAMS,
        name="fetch",
    )(side.reshape(1), lists, limits[None, :], table)


def row_sum_kernel(order, slot_ref, value_ref, out_ref):
    n = out_ref.shape[0]
    iota = lax.broadcasted_iota(jnp.int32, (n, LANES), 0)
    total = jnp.zeros(out_ref.shape, f32)
    for k in range(0, slot_ref.shape[0], 2):
        hot = jnp.concatenate(
            [jnp.where(slot_ref[j : j + 1, :] == iota, 1.0, 0.0).astype(bf16) for j in (k, k + 1)],
            axis=1,
        )
        values = value_ref[k * LANES : (k + 2) * LANES, :]
        total = total + jnp.dot(hot, values, preferred_element_type=f32)
    blocks = len(order)
    size = n // blocks
    for b, place in enumerate(order):
        out_ref[place * size : (place + 1) * size, :] = total[b * size : (b + 1) * size, :]


def row_sum(slot_rows, values, n, order):
    return pl.pallas_call(
        functools.partial(row_sum_kernel, order),
        out_shape=jax.ShapeDtypeStruct((n, values.shape[1]), f32),
        in_specs=[VMEM] * 2,
        out_specs=VMEM,
        compiler_params=PARAMS,
        name="row_sum",
    )(slot_rows, values)


def count_kernel(bag_ref, place_ref, out_ref):
    group, part = 32, 16
    one, zero = jnp.ones((), bf16), jnp.zeros((), bf16)

    def step(g, carry):
        rows = pl.ds(pl.multiple_of(g * group, group), group)
        bags = bag_ref[rows, :]
        names = [
            [
                jnp.broadcast_to(bags[p : p + part, l : l + 1], (part, LANES)).astype(jnp.int16)
                for l in range(bags.shape[1])
            ]
            for p in range(0, group, part)
        ]
        for t in range(out_ref.shape[1] // LANES):
            cols = slice(t * LANES, (t + 1) * LANES)
            place = jnp.broadcast_to(place_ref[0, :, cols], (part, LANES)).astype(jnp.int16)
            totals = []
            for part_names in names:
                total = jnp.zeros((part, LANES), bf16)
                for name in part_names:
                    total = total + jnp.where(name == place, one, zero)
                totals.append(total)
            out_ref[rows, cols] = jnp.concatenate(totals, axis=0).astype(out_ref.dtype)
        return carry

    lax.fori_loop(0, out_ref.shape[0] // group, step, 0)


def count(bags, places):
    n_bags, depth = bags.shape
    sides, _, slots = places.shape
    block = 128
    per = n_bags // sides // block
    return pl.pallas_call(
        count_kernel,
        grid=(n_bags // block,),
        out_shape=jax.ShapeDtypeStruct((n_bags, slots), jnp.float8_e4m3fn),
        in_specs=[
            pl.BlockSpec((block, depth), lambda i: (i, 0)),
            pl.BlockSpec((1, 1, slots), lambda i: (i // per, 0, 0)),
        ],
        out_specs=pl.BlockSpec((block, slots), lambda i: (i, 0)),
        compiler_params=PARAMS,
        cost_estimate=pl.CostEstimate(
            flops=n_bags * slots * depth * 2,
            bytes_accessed=n_bags * slots,
            transcendentals=0,
        ),
        name="count",
    )(bags, places)


def top_kernel(
    order,
    side_ref,
    here_ref,
    came_ref,
    w1_ref,
    b1_ref,
    w2_ref,
    label_ref,
    logit_ref,
    part_ref,
    g_ref,
):
    batch = logit_ref.shape[0]
    bags = here_ref.shape[0] // 2
    spans = [slice(f * batch, (f + 1) * batch) for f in range(bags // batch)]
    pooled = []
    for s in range(2):
        total = here_ref[s * bags : (s + 1) * bags, :] + came_ref[(1 - s) * bags : (2 - s) * bags, :]
        pooled.append(jnp.concatenate([total[span].astype(bf16) for span in spans], axis=1))
    pooled = jnp.concatenate(pooled, axis=0)
    w1 = w1_ref[...]
    pre = jnp.dot(pooled, w1, preferred_element_type=f32) + b1_ref[...]
    sig_pre = jax.nn.sigmoid(pre)
    active = pre * sig_pre
    w2 = w2_ref[...].astype(f32)
    logits = jnp.sum(active * w2, axis=1, keepdims=True)
    logit_ref[...] = logits[:batch]
    error = jax.nn.sigmoid(logits) - label_ref[...].astype(f32)
    part_w2 = jnp.sum(error * active, axis=0, keepdims=True)
    slope = sig_pre * (1.0 + pre * (1.0 - sig_pre))
    grad_pre = (error * w2 * slope).astype(bf16)
    grad_pooled = lax.dot_general(
        grad_pre, w1, (((1,), (1,)), ((), ())), preferred_element_type=f32
    )
    for s in range(2):
        for f, span in enumerate(spans):
            block = grad_pooled[s * batch : (s + 1) * batch, f * LANES : (f + 1) * LANES]
            g_ref[s * bags + span.start : s * bags + span.stop, :] = block.astype(bf16)
    half = pooled.shape[1] // 2
    chosen = jnp.where(side_ref[0] == 0, pooled[:, :half], pooled[:, half:])
    part_w1 = lax.dot_general(
        chosen, grad_pre, (((0,), (0,)), ((), ())), preferred_element_type=f32
    )
    depth, blocks = part_w1.shape[0] // len(order), part_w1.shape[1] // LANES
    pieces = part_ref.shape[1]
    each = blocks // pieces
    for c, place in enumerate(order):
        rows = part_w1[c * depth : (c + 1) * depth, :]
        for j in range(blocks):
            base = j % each * depth
            block = rows[:, j * LANES : (j + 1) * LANES]
            part_ref[place, j // each, base : base + depth, :] = block
        for p in range(pieces):
            part_ref[place, p, each * depth :, :] = jnp.zeros((blocks, LANES), f32)
    for j in range(blocks):
        row = each * depth + j
        part_ref[order[0], 0, row : row + 1, :] = part_w2[:, j * LANES : (j + 1) * LANES]


def top(side, here, came, w1, b1, w2, labels, order, pieces):
    batch = labels.shape[0] // 2
    chunks = len(order)
    blocks = w1.shape[1] // LANES
    depth = w1.size // 2 // chunks // pieces // LANES + blocks
    smem = pl.BlockSpec(memory_space=pltpu.SMEM)
    return pl.pallas_call(
        functools.partial(top_kernel, order),
        out_shape=(
            jax.ShapeDtypeStruct((batch, 1), f32),
            jax.ShapeDtypeStruct((chunks, pieces, depth, LANES), f32),
            jax.ShapeDtypeStruct(here.shape, bf16),
        ),
        in_specs=[smem] + [VMEM] * 6,
        out_specs=(VMEM,) * 3,
        compiler_params=PARAMS,
        name="top",
    )(side.reshape(1), here, came, w1, b1, w2, labels)


def update_kernel(
    parity_ref,
    mine_ref,
    other_ref,
    table_ref,
    accum_ref,
    accum_col_ref,
    new_table_ref,
    new_accum_ref,
    row_grad_ref,
    w1_grad_ref,
    w2_grad_ref,
):
    chips, depth, _ = mine_ref.shape
    rows, hidden = table_ref.shape[0], w1_grad_ref.shape[1]
    size, blocks = rows // (2 * chips), hidden // LANES
    each = blocks // NEAR
    chunk = w1_grad_ref.shape[0] // (2 * chips)
    first = parity_ref[0] == 0
    for y in range(chips):
        mine, other = mine_ref[y].astype(f32), other_ref[y].astype(f32)
        for c in range(2):
            got = jnp.where(first, mine, other) if c == 0 else jnp.where(first, other, mine)
            base = (chips * c + y) * chunk
            for j in range(blocks):
                at = j // each * (each * chunk + blocks) + j % each * chunk
                cols = slice(j * LANES, (j + 1) * LANES)
                w1_grad_ref[base : base + chunk, cols] = got[at : at + chunk, :]
            if y == 0 and c == 0:
                w2_grad_ref[...] = got[each * chunk : each * chunk + blocks, :]
            base = (2 * y + c) * size
            row_grad_ref[base : base + size, :] = got[depth - size :, :]
    grad = row_grad_ref[...]
    square = grad * grad
    means = []
    for i in range(rows // LANES):
        spread = lax.dot_general(
            jnp.full((8, LANES), 1.0 / LANES, f32),
            square[i * LANES : (i + 1) * LANES, :],
            (((1,), (1,)), ((), ())),
            precision=lax.Precision.HIGHEST,
            preferred_element_type=f32,
        )
        means.append(spread[:1, :])
    new_accum_ref[...] = accum_ref[...] + jnp.concatenate(means, axis=0)
    scale = accum_col_ref[...] + jnp.mean(square, axis=1, keepdims=True)
    new_table_ref[...] = table_ref[...] - LEARN_RATE * grad / jnp.sqrt(scale)


def update(mine, other, parity, table, accum, w1_shape):
    rows, width = table.shape
    blocks = w1_shape[1] // LANES
    smem = pl.BlockSpec(memory_space=pltpu.SMEM)
    new_table, new_accum, row_grad, w1_grad, w2_grad = pl.pallas_call(
        update_kernel,
        out_shape=(
            jax.ShapeDtypeStruct(table.shape, f32),
            jax.ShapeDtypeStruct((rows // LANES, LANES), f32),
            jax.ShapeDtypeStruct(table.shape, f32),
            jax.ShapeDtypeStruct(w1_shape, f32),
            jax.ShapeDtypeStruct((blocks, LANES), f32),
        ),
        in_specs=[smem] + [VMEM] * 5,
        out_specs=(VMEM,) * 5,
        compiler_params=PARAMS,
        name="update",
    )(parity.reshape(1), mine, other, table, accum.reshape(-1, LANES), accum[:, None])
    return new_table, new_accum.reshape(-1), row_grad, w1_grad, w2_grad.reshape(-1)


def side_of(index, bits):
    side = 0
    for b in bits:
        side = side ^ (index >> b & 1)
    return side


def swap(shard, mask, axis="reader"):
    pairs = [(i, i ^ mask) for i in range(lax.axis_size(axis))]
    return lax.ppermute(shard, axis, pairs)


def halve(blocks, sent_type, steps, axis="reader"):
    me = lax.axis_index(axis)
    for mask, bits in steps:
        half = blocks.shape[0] // 2
        side = side_of(me, bits)
        kept = lax.dynamic_slice_in_dim(blocks, side * half, half, 0)
        sent = lax.dynamic_slice_in_dim(blocks, (1 - side) * half, half, 0)
        blocks = kept + swap(sent.astype(sent_type), mask, axis).astype(f32)
    return blocks


def double(blocks, steps, axis):
    me = lax.axis_index(axis)
    for mask, bits in reversed(steps):
        came = swap(blocks, mask, axis)
        low = side_of(me, bits) == 0
        first, second = jnp.where(low, blocks, came), jnp.where(low, came, blocks)
        blocks = jnp.concatenate([first, second], axis=0)
    return blocks


def ring_steps(low, n):
    last = low + n - 1
    steps = [(1 << b, (b, last)) for b in range(low, last)]
    return steps + [(sum(1 << b for b in range(low, last + 1)), (last,))]


def places(steps, count):
    return [
        sum(side_of(i, bits) << (len(steps) - 1 - k) for k, (_, bits) in enumerate(steps))
        for i in range(count)
    ]


def partner(shard):
    return swap(shard, 1)


def exchange(blocks, axis, groups=None):
    return lax.all_to_all(
        blocks, axis, split_axis=0, concat_axis=0, tiled=True, axis_index_groups=groups
    )


def on_device(table, accum, serve, counts, slot_map, bag_rows, bag_len, labels, w1, b1, w2):
    lists = serve[0, 0]
    limits = counts[0, 0]
    n_peers, slots = lists.shape
    rows, width = table.shape
    half = slots // 2
    readers = lax.axis_size("reader")
    chips = readers // 2
    chip_bits = chips.bit_length() - 1
    chip_steps = ring_steps(1, chip_bits)
    near_steps = ring_steps(0, NEAR.bit_length() - 1)
    parity = lax.axis_index("reader") % 2
    own_lists = lax.dynamic_slice_in_dim(lists, parity * half, half, 1)
    own_slots = jnp.arange(half, dtype=jnp.int32)[None, :] + parity * half
    own_lists = jnp.where(own_slots < limits[:, None], own_lists, -1)
    slot_rows = own_lists.reshape(-1, LANES)
    picked = fetch(parity, lists, limits, table)
    fetched = exchange(picked.reshape(n_peers, half, width), "owner").reshape(-1, width)

    batch, feats, depth = bag_rows.shape
    inside = jnp.arange(depth, dtype=jnp.int32)[None, None, :] < bag_len[:, :, None]
    bags = jnp.where(inside, bag_rows, -1).transpose(1, 0, 2).reshape(-1, depth)
    cached = slot_map.reshape(n_peers, 2, half)
    own_places = lax.dynamic_slice_in_dim(cached, parity, 1, 1).reshape(-1)
    other_places = lax.dynamic_slice_in_dim(cached, 1 - parity, 1, 1).reshape(-1)
    sent = jnp.concatenate([bags.reshape(-1), other_places, labels]).reshape(-1, LANES)
    came = partner(sent).reshape(-1)
    came_bags = came[: bags.size].reshape(bags.shape)
    came_places = came[bags.size : -batch]
    both_labels = jnp.concatenate([labels, came[-batch:]])
    counted = count(
        jnp.concatenate([bags, came_bags], axis=0),
        jnp.stack([own_places, came_places])[:, None, :],
    )

    pooled = jnp.dot(counted.astype(bf16), fetched, preferred_element_type=f32)
    logits, part, grad_both = top(
        parity,
        pooled,
        partner(pooled),
        w1,
        b1[None, :],
        w2[None, :],
        both_labels[:, None],
        places(ring_steps(0, chip_bits), chips),
        NEAR,
    )
    slot_grad = lax.dot_general(
        counted.astype(bf16), grad_both, (((0,), (0,)), ((), ())), preferred_element_type=f32
    ).astype(bf16)

    part = halve(part, bf16, chip_steps[:1])
    part, slot_grad = lax.optimization_barrier((part, slot_grad))
    returned = exchange(slot_grad.reshape(n_peers, half, width), "owner").reshape(-1, width)
    part = halve(part, bf16, chip_steps[1:])[0]
    part = halve(part, f32, near_steps, "owner")[0].astype(bf16)
    part, returned = lax.optimization_barrier((part, returned))
    order = [b % 2 * chips + b // 2 for b in range(readers)]
    local_grad = row_sum(slot_rows, returned, rows, order)
    block = local_grad.reshape(readers, rows // readers, width)

    far = n_peers // NEAR
    part = jnp.broadcast_to(part[None], (far,) + part.shape)
    part = exchange(part, "owner", [list(range(x, n_peers, NEAR)) for x in range(NEAR)])
    chunk = jnp.sum(part.astype(f32), axis=0, keepdims=True).astype(bf16)
    block = halve(block, f32, [(1, (0,))])
    chunk, block = lax.optimization_barrier((chunk, block))
    same_core = [list(range(c, readers, 2)) for c in range(2)]
    block = jnp.sum(exchange(block, "reader", same_core), axis=0)
    chunk = double(chunk, near_steps, "owner").reshape(-1, LANES)
    mine = jnp.concatenate([chunk, block.astype(bf16)], axis=0)
    mine = jnp.broadcast_to(mine[None], (chips,) + mine.shape)
    mine = exchange(mine, "reader", same_core)
    new_table, new_accum, row_grad, w1_grad, w2_grad = update(
        mine, partner(mine), parity, table, accum, w1.shape
    )
    return (new_table, new_accum, row_grad, w1_grad, w2_grad, logits.reshape(-1))


def solution(mesh):
    return jax.shard_map(
        on_device,
        mesh=mesh,
        in_specs=(
            P("owner", None),
            P("owner"),
            P("owner", "reader", None, None),
            P("owner", "reader", None),
            P("owner", "reader", None),
            P(("owner", "reader"), None, None),
            P(("owner", "reader"), None),
            P(("owner", "reader")),
            P(),
            P(),
            P(),
        ),
        out_specs=(
            P("owner", None),
            P("owner"),
            P("owner", None),
            P(),
            P(),
            P(("owner", "reader")),
        ),
        check_vma=False,
    )
```

```python
import functools

import jax
import jax.numpy as jnp
from jax import lax
from jax.experimental import pallas as pl
from jax.experimental.pallas import tpu as pltpu
from jax.sharding import PartitionSpec as P

LEARN_RATE = 0.05
LANES = 128
NEAR = 4
bf16 = jnp.bfloat16
f32 = jnp.float32
VMEM = pl.BlockSpec(memory_space=pltpu.VMEM)
PARAMS = pltpu.CompilerParams(vmem_limit_bytes=48 * 1024 * 1024)


def fetch_kernel(side_ref, list_ref, limit_ref, table_ref, out_ref):
    table = table_ref[...].astype(bf16)
    peers = list_ref.shape[0]
    half = list_ref.shape[1] // 2
    lists = list_ref[...].T
    side = side_ref[0]
    lists = jnp.where(side == 0, lists[:half], lists[half:])
    slots = lax.broadcasted_iota(jnp.int32, (half, peers), 0) + side * half
    lists = jnp.where(slots < limit_ref[...], lists, -1)
    rows = lax.broadcasted_iota(jnp.int32, (half, table.shape[0]), 1)
    for p in range(0, peers, 2):
        hot = jnp.concatenate(
            [jnp.where(lists[:, q : q + 1] == rows, 1.0, 0.0).astype(bf16) for q in (p, p + 1)],
            axis=0,
        )
        picked = jnp.dot(hot, table, preferred_element_type=f32)
        out_ref[p * half : (p + 2) * half, :] = picked.astype(bf16)


def fetch(side, lists, limits, table):
    slots = lists.size // 2
    smem = pl.BlockSpec(memory_space=pltpu.SMEM)
    return pl.pallas_call(
        fetch_kernel,
        out_shape=jax.ShapeDtypeStruct((slots, table.shape[1]), bf16),
        in_specs=[smem] + [VMEM] * 3,
        out_specs=VMEM,
        compiler_params=PARAMS,
        name="fetch",
    )(side.reshape(1), lists, limits[None, :], table)


def row_sum_kernel(slot_ref, value_ref, out_ref):
    n = out_ref.shape[0]
    iota = lax.broadcasted_iota(jnp.int32, (n, LANES), 0)
    total = jnp.zeros(out_ref.shape, f32)
    for k in range(0, slot_ref.shape[0], 2):
        hot = jnp.concatenate(
            [jnp.where(slot_ref[j : j + 1, :] == iota, 1.0, 0.0).astype(bf16) for j in (k, k + 1)],
            axis=1,
        )
        values = value_ref[k * LANES : (k + 2) * LANES, :]
        total = total + jnp.dot(hot, values, preferred_element_type=f32)
    out_ref[...] = total


def row_sum(slot_rows, values, n):
    return pl.pallas_call(
        row_sum_kernel,
        out_shape=jax.ShapeDtypeStruct((n, values.shape[1]), f32),
        in_specs=[VMEM] * 2,
        out_specs=VMEM,
        compiler_params=PARAMS,
        name="row_sum",
    )(slot_rows, values)


def count_kernel(bag_ref, place_ref, out_ref):
    group, part = 32, 16
    one, zero = jnp.ones((), bf16), jnp.zeros((), bf16)

    def step(g, carry):
        rows = pl.ds(pl.multiple_of(g * group, group), group)
        bags = bag_ref[rows, :]
        names = [
            [
                jnp.broadcast_to(bags[p : p + part, l : l + 1], (part, LANES)).astype(jnp.int16)
                for l in range(bags.shape[1])
            ]
            for p in range(0, group, part)
        ]
        for t in range(out_ref.shape[1] // LANES):
            cols = slice(t * LANES, (t + 1) * LANES)
            place = jnp.broadcast_to(place_ref[0, :, cols], (part, LANES)).astype(jnp.int16)
            totals = []
            for part_names in names:
                total = jnp.zeros((part, LANES), bf16)
                for name in part_names:
                    total = total + jnp.where(name == place, one, zero)
                totals.append(total)
            out_ref[rows, cols] = jnp.concatenate(totals, axis=0).astype(out_ref.dtype)
        return carry

    lax.fori_loop(0, out_ref.shape[0] // group, step, 0)


def count(bags, places):
    n_bags, depth = bags.shape
    sides, _, slots = places.shape
    block = 128
    per = n_bags // sides // block
    return pl.pallas_call(
        count_kernel,
        grid=(n_bags // block,),
        out_shape=jax.ShapeDtypeStruct((n_bags, slots), jnp.float8_e4m3fn),
        in_specs=[
            pl.BlockSpec((block, depth), lambda i: (i, 0)),
            pl.BlockSpec((1, 1, slots), lambda i: (i // per, 0, 0)),
        ],
        out_specs=pl.BlockSpec((block, slots), lambda i: (i, 0)),
        compiler_params=PARAMS,
        cost_estimate=pl.CostEstimate(
            flops=n_bags * slots * depth * 2,
            bytes_accessed=n_bags * slots,
            transcendentals=0,
        ),
        name="count",
    )(bags, places)


def top_kernel(
    order,
    side_ref,
    here_ref,
    came_ref,
    w1_ref,
    b1_ref,
    w2_ref,
    label_ref,
    logit_ref,
    part_ref,
    g_ref,
):
    batch = logit_ref.shape[0]
    bags = here_ref.shape[0] // 2
    spans = [slice(f * batch, (f + 1) * batch) for f in range(bags // batch)]
    pooled = []
    for s in range(2):
        total = here_ref[s * bags : (s + 1) * bags, :] + came_ref[(1 - s) * bags : (2 - s) * bags, :]
        pooled.append(jnp.concatenate([total[span].astype(bf16) for span in spans], axis=1))
    pooled = jnp.concatenate(pooled, axis=0)
    w1 = w1_ref[...]
    pre = jnp.dot(pooled, w1, preferred_element_type=f32) + b1_ref[...]
    sig_pre = jax.nn.sigmoid(pre)
    active = pre * sig_pre
    w2 = w2_ref[...].astype(f32)
    logits = jnp.sum(active * w2, axis=1, keepdims=True)
    logit_ref[...] = logits[:batch]
    error = jax.nn.sigmoid(logits) - label_ref[...].astype(f32)
    part_w2 = jnp.sum(error * active, axis=0, keepdims=True)
    slope = sig_pre * (1.0 + pre * (1.0 - sig_pre))
    grad_pre = (error * w2 * slope).astype(bf16)
    grad_pooled = lax.dot_general(
        grad_pre, w1, (((1,), (1,)), ((), ())), preferred_element_type=f32
    )
    for s in range(2):
        for f, span in enumerate(spans):
            block = grad_pooled[s * batch : (s + 1) * batch, f * LANES : (f + 1) * LANES]
            g_ref[s * bags + span.start : s * bags + span.stop, :] = block.astype(bf16)
    half = pooled.shape[1] // 2
    chosen = jnp.where(side_ref[0] == 0, pooled[:, :half], pooled[:, half:])
    part_w1 = lax.dot_general(
        chosen, grad_pre, (((0,), (0,)), ((), ())), preferred_element_type=f32
    )
    depth, blocks = part_w1.shape[0] // len(order), part_w1.shape[1] // LANES
    pieces = part_ref.shape[1]
    each = blocks // pieces
    for c, place in enumerate(order):
        rows = part_w1[c * depth : (c + 1) * depth, :]
        for j in range(blocks):
            base = j % each * depth
            block = rows[:, j * LANES : (j + 1) * LANES]
            part_ref[place, j // each, base : base + depth, :] = block
        for p in range(pieces):
            part_ref[place, p, each * depth :, :] = jnp.zeros((blocks, LANES), f32)
    for j in range(blocks):
        row = each * depth + j
        part_ref[order[0], 0, row : row + 1, :] = part_w2[:, j * LANES : (j + 1) * LANES]


def top(side, here, came, w1, b1, w2, labels, order, pieces):
    batch = labels.shape[0] // 2
    chunks = len(order)
    blocks = w1.shape[1] // LANES
    depth = w1.size // 2 // chunks // pieces // LANES + blocks
    smem = pl.BlockSpec(memory_space=pltpu.SMEM)
    return pl.pallas_call(
        functools.partial(top_kernel, order),
        out_shape=(
            jax.ShapeDtypeStruct((batch, 1), f32),
            jax.ShapeDtypeStruct((chunks, pieces, depth, LANES), f32),
            jax.ShapeDtypeStruct(here.shape, bf16),
        ),
        in_specs=[smem] + [VMEM] * 6,
        out_specs=(VMEM,) * 3,
        compiler_params=PARAMS,
        name="top",
    )(side.reshape(1), here, came, w1, b1, w2, labels)


def update_kernel(
    parity_ref,
    mine_ref,
    other_ref,
    table_ref,
    accum_ref,
    accum_col_ref,
    new_table_ref,
    new_accum_ref,
    row_grad_ref,
    w1_grad_ref,
    w2_grad_ref,
):
    chips, depth, _ = mine_ref.shape
    rows, hidden = table_ref.shape[0], w1_grad_ref.shape[1]
    size, blocks = rows // (2 * chips), hidden // LANES
    each = blocks // NEAR
    chunk = w1_grad_ref.shape[0] // (2 * chips)
    first = parity_ref[0] == 0
    for y in range(chips):
        mine, other = mine_ref[y].astype(f32), other_ref[y].astype(f32)
        for c in range(2):
            got = jnp.where(first, mine, other) if c == 0 else jnp.where(first, other, mine)
            base = (chips * c + y) * chunk
            for j in range(blocks):
                at = j // each * (each * chunk + blocks) + j % each * chunk
                cols = slice(j * LANES, (j + 1) * LANES)
                w1_grad_ref[base : base + chunk, cols] = got[at : at + chunk, :]
            if y == 0 and c == 0:
                w2_grad_ref[...] = got[each * chunk : each * chunk + blocks, :]
            base = (2 * y + c) * size
            row_grad_ref[base : base + size, :] = got[depth - size :, :]
    grad = row_grad_ref[...]
    square = grad * grad
    means = []
    for i in range(rows // LANES):
        spread = lax.dot_general(
            jnp.full((8, LANES), 1.0 / LANES, f32),
            square[i * LANES : (i + 1) * LANES, :],
            (((1,), (1,)), ((), ())),
            precision=lax.Precision.HIGHEST,
            preferred_element_type=f32,
        )
        means.append(spread[:1, :])
    new_accum_ref[...] = accum_ref[...] + jnp.concatenate(means, axis=0)
    scale = accum_col_ref[...] + jnp.mean(square, axis=1, keepdims=True)
    new_table_ref[...] = table_ref[...] - LEARN_RATE * grad / jnp.sqrt(scale)


def update(mine, other, parity, table, accum, w1_shape):
    rows, width = table.shape
    blocks = w1_shape[1] // LANES
    smem = pl.BlockSpec(memory_space=pltpu.SMEM)
    new_table, new_accum, row_grad, w1_grad, w2_grad = pl.pallas_call(
        update_kernel,
        out_shape=(
            jax.ShapeDtypeStruct(table.shape, f32),
            jax.ShapeDtypeStruct((rows // LANES, LANES), f32),
            jax.ShapeDtypeStruct(table.shape, f32),
            jax.ShapeDtypeStruct(w1_shape, f32),
            jax.ShapeDtypeStruct((blocks, LANES), f32),
        ),
        in_specs=[smem] + [VMEM] * 5,
        out_specs=(VMEM,) * 5,
        compiler_params=PARAMS,
        name="update",
    )(parity.reshape(1), mine, other, table, accum.reshape(-1, LANES), accum[:, None])
    return new_table, new_accum.reshape(-1), row_grad, w1_grad, w2_grad.reshape(-1)


def side_of(index, bits):
    side = 0
    for b in bits:
        side = side ^ (index >> b & 1)
    return side


def swap(shard, mask, axis="reader"):
    pairs = [(i, i ^ mask) for i in range(lax.axis_size(axis))]
    return lax.ppermute(shard, axis, pairs)


def halve(blocks, sent_type, steps, axis="reader"):
    me = lax.axis_index(axis)
    for mask, bits in steps:
        half = blocks.shape[0] // 2
        side = side_of(me, bits)
        kept = lax.dynamic_slice_in_dim(blocks, side * half, half, 0)
        sent = lax.dynamic_slice_in_dim(blocks, (1 - side) * half, half, 0)
        blocks = kept + swap(sent.astype(sent_type), mask, axis).astype(f32)
    return blocks


def double(blocks, steps, axis):
    me = lax.axis_index(axis)
    for mask, bits in reversed(steps):
        came = swap(blocks, mask, axis)
        low = side_of(me, bits) == 0
        first, second = jnp.where(low, blocks, came), jnp.where(low, came, blocks)
        blocks = jnp.concatenate([first, second], axis=0)
    return blocks


def ring_steps(low, n):
    last = low + n - 1
    steps = [(1 << b, (b, last)) for b in range(low, last)]
    return steps + [(sum(1 << b for b in range(low, last + 1)), (last,))]


def places(steps, count):
    return [
        sum(side_of(i, bits) << (len(steps) - 1 - k) for k, (_, bits) in enumerate(steps))
        for i in range(count)
    ]


def partner(shard):
    return swap(shard, 1)


def exchange(blocks, axis, groups=None):
    return lax.all_to_all(
        blocks, axis, split_axis=0, concat_axis=0, tiled=True, axis_index_groups=groups
    )


def on_device(table, accum, serve, counts, slot_map, bag_rows, bag_len, labels, w1, b1, w2):
    lists = serve[0, 0]
    limits = counts[0, 0]
    n_peers, slots = lists.shape
    rows, width = table.shape
    half = slots // 2
    readers = lax.axis_size("reader")
    chips = readers // 2
    chip_bits = chips.bit_length() - 1
    chip_steps = ring_steps(1, chip_bits)
    near_steps = ring_steps(0, NEAR.bit_length() - 1)
    parity = lax.axis_index("reader") % 2
    own_lists = lax.dynamic_slice_in_dim(lists, parity * half, half, 1)
    own_slots = jnp.arange(half, dtype=jnp.int32)[None, :] + parity * half
    own_lists = jnp.where(own_slots < limits[:, None], own_lists, -1)
    slot_rows = own_lists.reshape(-1, LANES)
    picked = fetch(parity, lists, limits, table)
    fetched = exchange(picked.reshape(n_peers, half, width), "owner").reshape(-1, width)

    batch, feats, depth = bag_rows.shape
    inside = jnp.arange(depth, dtype=jnp.int32)[None, None, :] < bag_len[:, :, None]
    bags = jnp.where(inside, bag_rows, -1).transpose(1, 0, 2).reshape(-1, depth)
    cached = slot_map.reshape(n_peers, 2, half)
    own_places = lax.dynamic_slice_in_dim(cached, parity, 1, 1).reshape(-1)
    other_places = lax.dynamic_slice_in_dim(cached, 1 - parity, 1, 1).reshape(-1)
    sent = jnp.concatenate([bags.reshape(-1), other_places, labels]).reshape(-1, LANES)
    came = partner(sent).reshape(-1)
    came_bags = came[: bags.size].reshape(bags.shape)
    came_places = came[bags.size : -batch]
    both_labels = jnp.concatenate([labels, came[-batch:]])
    counted = count(
        jnp.concatenate([bags, came_bags], axis=0),
        jnp.stack([own_places, came_places])[:, None, :],
    )

    pooled = jnp.dot(counted.astype(bf16), fetched, preferred_element_type=f32)
    logits, part, grad_both = top(
        parity,
        pooled,
        partner(pooled),
        w1,
        b1[None, :],
        w2[None, :],
        both_labels[:, None],
        places(ring_steps(0, chip_bits), chips),
        NEAR,
    )
    slot_grad = lax.dot_general(
        counted.astype(bf16), grad_both, (((0,), (0,)), ((), ())), preferred_element_type=f32
    ).astype(bf16)

    part = halve(part, bf16, chip_steps[:1])
    part, slot_grad = lax.optimization_barrier((part, slot_grad))
    returned = exchange(slot_grad.reshape(n_peers, half, width), "owner").reshape(-1, width)
    part = halve(part, bf16, chip_steps[1:])[0]
    part = halve(part, f32, near_steps, "owner")[0].astype(bf16)
    part, returned = lax.optimization_barrier((part, returned))
    local_grad = row_sum(slot_rows, returned, rows)
    block = local_grad.reshape(readers, rows // readers, width)

    far = n_peers // NEAR
    part = jnp.broadcast_to(part[None], (far,) + part.shape)
    part = exchange(part, "owner", [list(range(x, n_peers, NEAR)) for x in range(NEAR)])
    chunk = jnp.sum(part.astype(f32), axis=0, keepdims=True).astype(bf16)
    chunk, block = lax.optimization_barrier((chunk, block))
    same_core = [list(range(c, readers, 2)) for c in range(2)]
    block = jnp.sum(exchange(block, "reader"), axis=0)
    chunk = double(chunk, near_steps, "owner").reshape(-1, LANES)
    mine = jnp.concatenate([chunk, block.astype(bf16)], axis=0)
    mine = jnp.broadcast_to(mine[None], (chips,) + mine.shape)
    mine = exchange(mine, "reader", same_core)
    new_table, new_accum, row_grad, w1_grad, w2_grad = update(
        mine, partner(mine), parity, table, accum, w1.shape
    )
    return (new_table, new_accum, row_grad, w1_grad, w2_grad, logits.reshape(-1))


def solution(mesh):
    return jax.shard_map(
        on_device,
        mesh=mesh,
        in_specs=(
            P("owner", None),
            P("owner"),
            P("owner", "reader", None, None),
            P("owner", "reader", None),
            P("owner", "reader", None),
            P(("owner", "reader"), None, None),
            P(("owner", "reader"), None),
            P(("owner", "reader")),
            P(),
            P(),
            P(),
        ),
        out_specs=(
            P("owner", None),
            P("owner"),
            P("owner", None),
            P(),
            P(),
            P(("owner", "reader")),
        ),
        check_vma=False,
    )
```

```python
import functools

import jax
import jax.numpy as jnp
from jax import lax
from jax.experimental import pallas as pl
from jax.experimental.pallas import tpu as pltpu
from jax.sharding import PartitionSpec as P

LEARN_RATE = 0.05
LANES = 128
NEAR = 4
bf16 = jnp.bfloat16
f32 = jnp.float32
VMEM = pl.BlockSpec(memory_space=pltpu.VMEM)
PARAMS = pltpu.CompilerParams(vmem_limit_bytes=48 * 1024 * 1024)


def fetch_kernel(
    side_ref, list_hbm, limit_ref, table_hbm, out_ref, list_ref, table_ref, list_sem, table_sem
):
    list_copy = pltpu.make_async_copy(list_hbm, list_ref, list_sem)
    table_copy = pltpu.make_async_copy(table_hbm, table_ref, table_sem)
    list_copy.start()
    table_copy.start()
    peers = list_ref.shape[0]
    half = list_ref.shape[1] // 2
    list_copy.wait()
    lists = list_ref[...].T
    side = side_ref[0]
    lists = jnp.where(side == 0, lists[:half], lists[half:])
    slots = lax.broadcasted_iota(jnp.int32, (half, peers), 0) + side * half
    lists = jnp.where(slots < limit_ref[...], lists, -1)
    table_copy.wait()
    table = table_ref[...].astype(bf16)
    rows = lax.broadcasted_iota(jnp.int32, (half, table.shape[0]), 1)
    for p in range(0, peers, 2):
        hot = jnp.concatenate(
            [jnp.where(lists[:, q : q + 1] == rows, 1.0, 0.0).astype(bf16) for q in (p, p + 1)],
            axis=0,
        )
        picked = jnp.dot(hot, table, preferred_element_type=f32)
        out_ref[p * half : (p + 2) * half, :] = picked.astype(bf16)


def fetch(side, lists, limits, table):
    slots = lists.size // 2
    smem = pl.BlockSpec(memory_space=pltpu.SMEM)
    anywhere = pl.BlockSpec(memory_space=pl.ANY)
    return pl.pallas_call(
        fetch_kernel,
        out_shape=jax.ShapeDtypeStruct((slots, table.shape[1]), bf16),
        in_specs=[smem, anywhere, VMEM, anywhere],
        out_specs=VMEM,
        scratch_shapes=[
            pltpu.VMEM(lists.shape, lists.dtype),
            pltpu.VMEM(table.shape, table.dtype),
            pltpu.SemaphoreType.DMA(()),
            pltpu.SemaphoreType.DMA(()),
        ],
        compiler_params=PARAMS,
        name="fetch",
    )(side.reshape(1), lists, limits[None, :], table)


def row_sum_kernel(order, slot_ref, value_ref, out_ref):
    n = out_ref.shape[0]
    iota = lax.broadcasted_iota(jnp.int32, (n, LANES), 0)
    total = jnp.zeros(out_ref.shape, f32)
    for k in range(0, slot_ref.shape[0], 2):
        hot = jnp.concatenate(
            [jnp.where(slot_ref[j : j + 1, :] == iota, 1.0, 0.0).astype(bf16) for j in (k, k + 1)],
            axis=1,
        )
        values = value_ref[k * LANES : (k + 2) * LANES, :]
        total = total + jnp.dot(hot, values, preferred_element_type=f32)
    blocks = len(order)
    size = n // blocks
    for b, place in enumerate(order):
        out_ref[place * size : (place + 1) * size, :] = total[b * size : (b + 1) * size, :]


def row_sum(slot_rows, values, n, order):
    return pl.pallas_call(
        functools.partial(row_sum_kernel, order),
        out_shape=jax.ShapeDtypeStruct((n, values.shape[1]), f32),
        in_specs=[VMEM] * 2,
        out_specs=VMEM,
        compiler_params=PARAMS,
        name="row_sum",
    )(slot_rows, values)


def count_kernel(bag_ref, place_ref, out_ref):
    group, part = 32, 16
    one, zero = jnp.ones((), bf16), jnp.zeros((), bf16)

    def step(g, carry):
        rows = pl.ds(pl.multiple_of(g * group, group), group)
        bags = bag_ref[rows, :]
        names = [
            [
                jnp.broadcast_to(bags[p : p + part, l : l + 1], (part, LANES)).astype(jnp.int16)
                for l in range(bags.shape[1])
            ]
            for p in range(0, group, part)
        ]
        for t in range(out_ref.shape[1] // LANES):
            cols = slice(t * LANES, (t + 1) * LANES)
            place = jnp.broadcast_to(place_ref[0, :, cols], (part, LANES)).astype(jnp.int16)
            totals = []
            for part_names in names:
                total = jnp.zeros((part, LANES), bf16)
                for name in part_names:
                    total = total + jnp.where(name == place, one, zero)
                totals.append(total)
            out_ref[rows, cols] = jnp.concatenate(totals, axis=0).astype(out_ref.dtype)
        return carry

    lax.fori_loop(0, out_ref.shape[0] // group, step, 0)


def count(bags, places):
    n_bags, depth = bags.shape
    sides, _, slots = places.shape
    block = 128
    per = n_bags // sides // block
    return pl.pallas_call(
        count_kernel,
        grid=(n_bags // block,),
        out_shape=jax.ShapeDtypeStruct((n_bags, slots), jnp.float8_e4m3fn),
        in_specs=[
            pl.BlockSpec((block, depth), lambda i: (i, 0)),
            pl.BlockSpec((1, 1, slots), lambda i: (i // per, 0, 0)),
        ],
        out_specs=pl.BlockSpec((block, slots), lambda i: (i, 0)),
        compiler_params=PARAMS,
        cost_estimate=pl.CostEstimate(
            flops=n_bags * slots * depth * 2,
            bytes_accessed=n_bags * slots,
            transcendentals=0,
        ),
        name="count",
    )(bags, places)


def top_kernel(
    order,
    side_ref,
    here_ref,
    came_ref,
    w1_ref,
    b1_ref,
    w2_ref,
    label_ref,
    logit_ref,
    part_ref,
    g_ref,
):
    batch = logit_ref.shape[0]
    bags = here_ref.shape[0] // 2
    spans = [slice(f * batch, (f + 1) * batch) for f in range(bags // batch)]
    pooled = []
    for s in range(2):
        total = here_ref[s * bags : (s + 1) * bags, :] + came_ref[(1 - s) * bags : (2 - s) * bags, :]
        pooled.append(jnp.concatenate([total[span].astype(bf16) for span in spans], axis=1))
    pooled = jnp.concatenate(pooled, axis=0)
    w1 = w1_ref[...]
    pre = jnp.dot(pooled, w1, preferred_element_type=f32) + b1_ref[...]
    sig_pre = jax.nn.sigmoid(pre)
    active = pre * sig_pre
    w2 = w2_ref[...].astype(f32)
    logits = jnp.sum(active * w2, axis=1, keepdims=True)
    logit_ref[...] = logits[:batch]
    error = jax.nn.sigmoid(logits) - label_ref[...].astype(f32)
    part_w2 = jnp.sum(error * active, axis=0, keepdims=True)
    slope = sig_pre * (1.0 + pre * (1.0 - sig_pre))
    grad_pre = (error * w2 * slope).astype(bf16)
    grad_pooled = lax.dot_general(
        grad_pre, w1, (((1,), (1,)), ((), ())), preferred_element_type=f32
    )
    for s in range(2):
        for f, span in enumerate(spans):
            block = grad_pooled[s * batch : (s + 1) * batch, f * LANES : (f + 1) * LANES]
            g_ref[s * bags + span.start : s * bags + span.stop, :] = block.astype(bf16)
    half = pooled.shape[1] // 2
    chosen = jnp.where(side_ref[0] == 0, pooled[:, :half], pooled[:, half:])
    part_w1 = lax.dot_general(
        chosen, grad_pre, (((0,), (0,)), ((), ())), preferred_element_type=f32
    )
    depth, blocks = part_w1.shape[0] // len(order), part_w1.shape[1] // LANES
    pieces = part_ref.shape[1]
    each = blocks // pieces
    for c, place in enumerate(order):
        rows = part_w1[c * depth : (c + 1) * depth, :]
        for j in range(blocks):
            base = j % each * depth
            block = rows[:, j * LANES : (j + 1) * LANES]
            part_ref[place, j // each, base : base + depth, :] = block
        for p in range(pieces):
            part_ref[place, p, each * depth :, :] = jnp.zeros((blocks, LANES), f32)
    for j in range(blocks):
        row = each * depth + j
        part_ref[order[0], 0, row : row + 1, :] = part_w2[:, j * LANES : (j + 1) * LANES]


def top(side, here, came, w1, b1, w2, labels, order, pieces):
    batch = labels.shape[0] // 2
    chunks = len(order)
    blocks = w1.shape[1] // LANES
    depth = w1.size // 2 // chunks // pieces // LANES + blocks
    smem = pl.BlockSpec(memory_space=pltpu.SMEM)
    return pl.pallas_call(
        functools.partial(top_kernel, order),
        out_shape=(
            jax.ShapeDtypeStruct((batch, 1), f32),
            jax.ShapeDtypeStruct((chunks, pieces, depth, LANES), f32),
            jax.ShapeDtypeStruct(here.shape, bf16),
        ),
        in_specs=[smem] + [VMEM] * 6,
        out_specs=(VMEM,) * 3,
        compiler_params=PARAMS,
        name="top",
    )(side.reshape(1), here, came, w1, b1, w2, labels)


def update_kernel(
    parity_ref,
    mine_ref,
    other_ref,
    table_ref,
    accum_ref,
    accum_col_ref,
    new_table_ref,
    new_accum_ref,
    row_grad_ref,
    w1_grad_ref,
    w2_grad_ref,
):
    chips, depth, _ = mine_ref.shape
    rows, hidden = table_ref.shape[0], w1_grad_ref.shape[1]
    size, blocks = rows // (2 * chips), hidden // LANES
    each = blocks // NEAR
    chunk = w1_grad_ref.shape[0] // (2 * chips)
    first = parity_ref[0] == 0
    for y in range(chips):
        mine, other = mine_ref[y].astype(f32), other_ref[y].astype(f32)
        for c in range(2):
            got = jnp.where(first, mine, other) if c == 0 else jnp.where(first, other, mine)
            base = (chips * c + y) * chunk
            for j in range(blocks):
                at = j // each * (each * chunk + blocks) + j % each * chunk
                cols = slice(j * LANES, (j + 1) * LANES)
                w1_grad_ref[base : base + chunk, cols] = got[at : at + chunk, :]
            if y == 0 and c == 0:
                w2_grad_ref[...] = got[each * chunk : each * chunk + blocks, :]
            base = (2 * y + c) * size
            row_grad_ref[base : base + size, :] = got[depth - size :, :]
    grad = row_grad_ref[...]
    square = grad * grad
    means = []
    for i in range(rows // LANES):
        spread = lax.dot_general(
            jnp.full((8, LANES), 1.0 / LANES, f32),
            square[i * LANES : (i + 1) * LANES, :],
            (((1,), (1,)), ((), ())),
            precision=lax.Precision.HIGHEST,
            preferred_element_type=f32,
        )
        means.append(spread[:1, :])
    new_accum_ref[...] = accum_ref[...] + jnp.concatenate(means, axis=0)
    scale = accum_col_ref[...] + jnp.mean(square, axis=1, keepdims=True)
    new_table_ref[...] = table_ref[...] - LEARN_RATE * grad / jnp.sqrt(scale)


def update(mine, other, parity, table, accum, w1_shape):
    rows, width = table.shape
    blocks = w1_shape[1] // LANES
    smem = pl.BlockSpec(memory_space=pltpu.SMEM)
    new_table, new_accum, row_grad, w1_grad, w2_grad = pl.pallas_call(
        update_kernel,
        out_shape=(
            jax.ShapeDtypeStruct(table.shape, f32),
            jax.ShapeDtypeStruct((rows // LANES, LANES), f32),
            jax.ShapeDtypeStruct(table.shape, f32),
            jax.ShapeDtypeStruct(w1_shape, f32),
            jax.ShapeDtypeStruct((blocks, LANES), f32),
        ),
        in_specs=[smem] + [VMEM] * 5,
        out_specs=(VMEM,) * 5,
        compiler_params=PARAMS,
        name="update",
    )(parity.reshape(1), mine, other, table, accum.reshape(-1, LANES), accum[:, None])
    return new_table, new_accum.reshape(-1), row_grad, w1_grad, w2_grad.reshape(-1)


def side_of(index, bits):
    side = 0
    for b in bits:
        side = side ^ (index >> b & 1)
    return side


def swap(shard, mask, axis="reader"):
    pairs = [(i, i ^ mask) for i in range(lax.axis_size(axis))]
    return lax.ppermute(shard, axis, pairs)


def halve(blocks, sent_type, steps, axis="reader"):
    me = lax.axis_index(axis)
    for mask, bits in steps:
        half = blocks.shape[0] // 2
        side = side_of(me, bits)
        kept = lax.dynamic_slice_in_dim(blocks, side * half, half, 0)
        sent = lax.dynamic_slice_in_dim(blocks, (1 - side) * half, half, 0)
        blocks = kept + swap(sent.astype(sent_type), mask, axis).astype(f32)
    return blocks


def double(blocks, steps, axis):
    me = lax.axis_index(axis)
    for mask, bits in reversed(steps):
        came = swap(blocks, mask, axis)
        low = side_of(me, bits) == 0
        first, second = jnp.where(low, blocks, came), jnp.where(low, came, blocks)
        blocks = jnp.concatenate([first, second], axis=0)
    return blocks


def ring_steps(low, n):
    last = low + n - 1
    steps = [(1 << b, (b, last)) for b in range(low, last)]
    return steps + [(sum(1 << b for b in range(low, last + 1)), (last,))]


def places(steps, count):
    return [
        sum(side_of(i, bits) << (len(steps) - 1 - k) for k, (_, bits) in enumerate(steps))
        for i in range(count)
    ]


def partner(shard):
    return swap(shard, 1)


def exchange(blocks, axis, groups=None):
    return lax.all_to_all(
        blocks, axis, split_axis=0, concat_axis=0, tiled=True, axis_index_groups=groups
    )


def on_device(table, accum, serve, counts, slot_map, bag_rows, bag_len, labels, w1, b1, w2):
    lists = serve[0, 0]
    limits = counts[0, 0]
    n_peers, slots = lists.shape
    rows, width = table.shape
    half = slots // 2
    readers = lax.axis_size("reader")
    chips = readers // 2
    chip_bits = chips.bit_length() - 1
    chip_steps = ring_steps(1, chip_bits)
    near_steps = ring_steps(0, NEAR.bit_length() - 1)
    parity = lax.axis_index("reader") % 2
    own_lists = lax.dynamic_slice_in_dim(lists, parity * half, half, 1)
    own_slots = jnp.arange(half, dtype=jnp.int32)[None, :] + parity * half
    own_lists = jnp.where(own_slots < limits[:, None], own_lists, -1)
    slot_rows = own_lists.reshape(-1, LANES)
    picked = fetch(parity, lists, limits, table)
    fetched = exchange(picked.reshape(n_peers, half, width), "owner").reshape(-1, width)

    batch, feats, depth = bag_rows.shape
    inside = jnp.arange(depth, dtype=jnp.int32)[None, None, :] < bag_len[:, :, None]
    bags = jnp.where(inside, bag_rows, -1).transpose(1, 0, 2).reshape(-1, depth)
    cached = slot_map.reshape(n_peers, 2, half)
    own_places = lax.dynamic_slice_in_dim(cached, parity, 1, 1).reshape(-1)
    other_places = lax.dynamic_slice_in_dim(cached, 1 - parity, 1, 1).reshape(-1)
    sent = jnp.concatenate([bags.reshape(-1), other_places, labels]).reshape(-1, LANES)
    came = partner(sent).reshape(-1)
    came_bags = came[: bags.size].reshape(bags.shape)
    came_places = came[bags.size : -batch]
    both_labels = jnp.concatenate([labels, came[-batch:]])
    counted = count(
        jnp.concatenate([bags, came_bags], axis=0),
        jnp.stack([own_places, came_places])[:, None, :],
    )

    pooled = jnp.dot(counted.astype(bf16), fetched, preferred_element_type=f32)
    logits, part, grad_both = top(
        parity,
        pooled,
        partner(pooled),
        w1,
        b1[None, :],
        w2[None, :],
        both_labels[:, None],
        places(ring_steps(0, chip_bits), chips),
        NEAR,
    )
    slot_grad = lax.dot_general(
        counted.astype(bf16), grad_both, (((0,), (0,)), ((), ())), preferred_element_type=f32
    ).astype(bf16)

    part = halve(part, bf16, chip_steps[:1])
    part, slot_grad = lax.optimization_barrier((part, slot_grad))
    returned = exchange(slot_grad.reshape(n_peers, half, width), "owner").reshape(-1, width)
    part = halve(part, bf16, chip_steps[1:])[0]
    part = halve(part, f32, near_steps, "owner")[0].astype(bf16)
    part, returned = lax.optimization_barrier((part, returned))
    order = [b % 2 * chips + b // 2 for b in range(readers)]
    local_grad = row_sum(slot_rows, returned, rows, order)
    block = local_grad.reshape(readers, rows // readers, width)

    far = n_peers // NEAR
    part = jnp.broadcast_to(part[None], (far,) + part.shape)
    part = exchange(part, "owner", [list(range(x, n_peers, NEAR)) for x in range(NEAR)])
    chunk = jnp.sum(part.astype(f32), axis=0, keepdims=True).astype(bf16)
    block = halve(block, f32, [(1, (0,))])
    chunk, block = lax.optimization_barrier((chunk, block))
    same_core = [list(range(c, readers, 2)) for c in range(2)]
    block = jnp.sum(exchange(block, "reader", same_core), axis=0)
    chunk = double(chunk, near_steps, "owner").reshape(-1, LANES)
    mine = jnp.concatenate([chunk, block.astype(bf16)], axis=0)
    mine = jnp.broadcast_to(mine[None], (chips,) + mine.shape)
    mine = exchange(mine, "reader", same_core)
    new_table, new_accum, row_grad, w1_grad, w2_grad = update(
        mine, partner(mine), parity, table, accum, w1.shape
    )
    return (new_table, new_accum, row_grad, w1_grad, w2_grad, logits.reshape(-1))


def solution(mesh):
    return jax.shard_map(
        on_device,
        mesh=mesh,
        in_specs=(
            P("owner", None),
            P("owner"),
            P("owner", "reader", None, None),
            P("owner", "reader", None),
            P("owner", "reader", None),
            P(("owner", "reader"), None, None),
            P(("owner", "reader"), None),
            P(("owner", "reader")),
            P(),
            P(),
            P(),
        ),
        out_specs=(
            P("owner", None),
            P("owner"),
            P("owner", None),
            P(),
            P(),
            P(("owner", "reader")),
        ),
        check_vma=False,
    )
```
